32 devices in a mesh: dp: 8 (over y, x, core), tensor: 4 (over z).
Axes of the slice: x: 2, y: 2, z: 4, core: 2. Of those that a mesh axis runs over, the one named last changes fastest.
Arguments:
- tokens: bfloat16 [8192, 2048], P(('dp', 'tensor')), may hold values from -6 to 6
- cotangent: bfloat16 [8192, 2048], P(('dp', 'tensor')), may hold values from -6 to 6
- doc_start: int32 [8192], P('dp'), may hold values from 0 to 1023, as said below
- in_weight: float32 [2048, 3, 2048], P('dp', None, 'tensor'), may hold values from -0.125 to 0.125
- in_first: float32 [2048, 3, 2048], P('dp', None, 'tensor'), may hold values from -32 to 32
- in_second: float32 [2048, 3, 2048], P('dp', None, 'tensor'), may hold values from 106.496 to 434.176
- out_weight: float32 [2048, 2048], P('tensor', 'dp'), may hold values from -0.375 to 0.375
- out_first: float32 [2048, 2048], P('tensor', 'dp'), may hold values from -16 to 16
- out_second: float32 [2048, 2048], P('tensor', 'dp'), may hold values from 27.0336 to 106.496
- gate_up: float32 [2048, 2, 8192], P('dp', None, 'tensor'), may hold values from -0.125 to 0.125
- gate_up_first: float32 [2048, 2, 8192], P('dp', None, 'tensor'), may hold values from -16 to 16
- gate_up_second: float32 [2048, 2, 8192], P('dp', None, 'tensor'), may hold values from 38.5024 to 155.648
- down_weight: float32 [8192, 2048], P('tensor', 'dp'), may hold values from -0.0625 to 0.0625
- down_first: float32 [8192, 2048], P('tensor', 'dp'), may hold values from -32 to 32
- down_second: float32 [8192, 2048], P('tensor', 'dp'), may hold values from 155.648 to 622.592
- norm_gains: float32 [2, 2048], P(None, 'dp'), may hold values from 0.5 to 1.5
- gains_first: float32 [2, 2048], P(None, 'dp'), may hold values from -56 to 56
- gains_second: float32 [2, 2048], P(None, 'dp'), may hold values from 352.256 to 1392.64
Outputs:
- output: bfloat16 [8192, 2048], P(('dp', 'tensor'))
- input_grad: float32 [8192, 2048], P(('dp', 'tensor'))
- new_in_first: float32 [2048, 3, 2048], P('dp', None, 'tensor')
- new_in_second: float32 [2048, 3, 2048], P('dp', None, 'tensor')
- new_in_weight: float32 [2048, 3, 2048], P('dp', None, 'tensor')
- new_out_first: float32 [2048, 2048], P('tensor', 'dp')
- new_out_second: float32 [2048, 2048], P('tensor', 'dp')
- new_out_weight: float32 [2048, 2048], P('tensor', 'dp')
- new_gate_up_first: float32 [2048, 2, 8192], P('dp', None, 'tensor')
- new_gate_up_second: float32 [2048, 2, 8192], P('dp', None, 'tensor')
- new_gate_up: float32 [2048, 2, 8192], P('dp', None, 'tensor')
- new_down_first: float32 [8192, 2048], P('tensor', 'dp')
- new_down_second: float32 [8192, 2048], P('tensor', 'dp')
- new_down_weight: float32 [8192, 2048], P('tensor', 'dp')
- new_gains_first: float32 [2, 2048], P(None, 'dp')
- new_gains_second: float32 [2, 2048], P(None, 'dp')
- new_norm_gains: float32 [2, 2048], P(None, 'dp')
The draws below stay inside these ranges and needn't reach their ends.
Inputs may be any that keep to these rules, and one draw needn't show every extreme that they name: doc_start[t] is the slot, counted from 0 within t's data group of 1024 consecutive tokens, of the first token of t's document: within a group values never fall and each equals the slot at which it first appears, so documents are runs of equal values; one data group holds a single document of 1024 tokens.
All inputs are finite; a program needn't handle non-finite values.
Results may differ from the reference program's by a relative error of at most 0.028.
Values may be sent and summed in bfloat16 or wider, within the bound.
A program may use at most 320 MiB of HBM per device.

```python
import math
import jax
import jax.numpy as jnp
from jax import lax

D = 2048
HEADS = 32
HEAD_DIM = 64
FF = 8192
TOK_DEV = 1024
STEP = 5
TOKENS = 8192
N_DP = 8


def draw_doc_start(key, part):
    key = jax.random.fold_in(key, 7)
    key_rate, key_roll, key_pick = jax.random.split(key, 3)
    groups = TOKENS // TOK_DEV
    spacing = jax.random.randint(key_rate, (groups, 1), 4, max(8, TOK_DEV // 2), dtype=jnp.int32)
    rolls = jax.random.randint(key_roll, (groups, TOK_DEV), 0, 1 << 20, dtype=jnp.int32)
    slots = jnp.arange(TOK_DEV, dtype=jnp.int32)[None, :]
    group_ids = jnp.arange(groups, dtype=jnp.int32)[:, None]
    whole_group = jax.random.randint(key_pick, (), 0, groups, dtype=jnp.int32)
    short_group = (whole_group + 1) % groups
    begins = (rolls % spacing == 0) | (slots == 0)
    begins = jnp.where(group_ids == whole_group, slots == 0, begins)
    begins = jnp.where((group_ids == short_group) & (slots == TOK_DEV - 1), True, begins)
    marked = jnp.where(begins, slots, 0)
    return lax.cummax(marked, axis=1).reshape(-1)


def raised(array, rng, source, target, parts, factor):
    owner, partner = [(jnp.arange(array.shape[dim]) // (array.shape[dim] // parts)).reshape([-1 if axis == dim else 1 for axis in range(array.ndim)]) for dim in (source, target)]
    chosen = jax.random.permutation(rng, parts)[partner]
    strong = (owner == chosen) | (owner == (partner + parts // 2) % parts)
    return jnp.where(strong, factor * array, array)


def block_scale(stream_key, shape, shards, smallest, largest):
    def one(dim, blocks):
        steps = jax.random.uniform(jax.random.fold_in(jax.random.fold_in(stream_key, 6), dim), (blocks,), jnp.float32, smallest / len(shards), largest / len(shards))
        return jnp.repeat(jnp.exp(steps), shape[dim] // blocks).reshape((-1,) + (1,) * (len(shape) - dim - 1))

    factor_of = one(*shards[0])
    for cut in shards[1:]:
        factor_of = factor_of * one(*cut)
    return factor_of


def bell_draw(stream_key, dims, width, bound, pieces=(), kind=jnp.bfloat16):
    values = width * jax.random.normal(stream_key, dims, jnp.float32)
    if pieces:
        values = values * block_scale(stream_key, dims, pieces, -0.22, 0.18)
    return jnp.clip(values, -bound, bound).astype(kind)


def noise_with(key, extent, scale, reach, shards, heavy, held_as=jnp.bfloat16):
    values = scale * jax.random.normal(key, extent, jnp.float32)
    if shards:
        values = values * block_scale(key, extent, shards, -0.22, 0.18)
    return jnp.clip(raised(values, jax.random.fold_in(key, 3), *heavy), -reach, reach).astype(held_as)


def setup_inputs(seed: int = 0) -> dict:
    key_of = jax.random.split(jax.random.key(seed), 19)
    tokens = bell_draw(key_of[0], (TOKENS, D), 1.0, 6.0, ((0, 32),))
    cotangent = noise_with(key_of[1], (TOKENS, D), 1.0, 6.0, ((0, 32),), (0, 1, 32, 2.75))
    doc_start = draw_doc_start(jax.random.fold_in(key_of[18], 71), 0)
    in_weight = bell_draw(key_of[3], (D, 3, D), D ** -0.5, 0.125, ((0, 8), (2, 4)), jnp.float32)
    in_first = bell_draw(key_of[4], (D, 3, D), (0.055 * TOKENS ** 0.5), 32.0, ((0, 8), (2, 4)), jnp.float32)
    in_second = jnp.clip(jnp.exp(math.log(434.176) - 1.40534252 * jax.random.uniform(key_of[5], (D, 3, D), jnp.float32) ** block_scale(key_of[5], (D, 3, D), ((0, 8), (2, 4)), -0.2, 0.2)), 106.496, 434.176)
    out_weight = bell_draw(key_of[6], (D, D), (D // 8) ** -0.5, 0.375, ((0, 4), (1, 8)), jnp.float32)
    out_first = bell_draw(key_of[7], (D, D), (0.028 * TOKENS ** 0.5), 16.0, ((0, 4), (1, 8)), jnp.float32)
    out_second = jnp.clip(jnp.exp(math.log(106.496) - 1.3710269 * jax.random.uniform(key_of[8], (D, D), jnp.float32) ** block_scale(key_of[8], (D, D), ((0, 4), (1, 8)), -0.2, 0.2)), 27.0336, 106.496)
    gate_up = bell_draw(key_of[9], (D, 2, FF), D ** -0.5, 0.125, ((0, 8), (2, 4)), jnp.float32)
    gate_up_first = bell_draw(key_of[10], (D, 2, FF), (0.033 * TOKENS ** 0.5), 16.0, ((0, 8), (2, 4)), jnp.float32)
    gate_up_second = jnp.clip(jnp.exp(math.log(155.648) - 1.3968765 * jax.random.uniform(key_of[11], (D, 2, FF), jnp.float32) ** block_scale(key_of[11], (D, 2, FF), ((0, 8), (2, 4)), -0.2, 0.2)), 38.5024, 155.648)
    down_weight = bell_draw(key_of[12], (FF, D), FF ** -0.5, 0.0625, ((0, 4), (1, 8)), jnp.float32)
    down_first = bell_draw(key_of[13], (FF, D), (0.067 * TOKENS ** 0.5), 32.0, ((0, 4), (1, 8)), jnp.float32)
    down_second = jnp.clip(jnp.exp(math.log(622.592) - 1.3862944 * jax.random.uniform(key_of[14], (FF, D), jnp.float32) ** block_scale(key_of[14], (FF, D), ((0, 4), (1, 8)), -0.2, 0.2)), 155.648, 622.592)
    norm_gains = jnp.clip(1.0 + 0.1 * jax.random.normal(key_of[15], (2, D), jnp.float32), 0.5, 1.5)
    gains_first = bell_draw(key_of[16], (2, D), (0.1 * TOKENS ** 0.5), 56.0, ((1, 8),), jnp.float32)
    gains_second = jnp.clip(jnp.exp(math.log(1392.64) - 1.3745983 * jax.random.uniform(key_of[17], (2, D), jnp.float32) ** block_scale(key_of[17], (2, D), ((1, 8),), -0.2, 0.2)), 352.256, 1392.64)
    return {"tokens": tokens, "cotangent": cotangent, "doc_start": doc_start, "in_weight": in_weight, "in_first": in_first, "in_second": in_second, "out_weight": out_weight, "out_first": out_first, "out_second": out_second, "gate_up": gate_up, "gate_up_first": gate_up_first, "gate_up_second": gate_up_second, "down_weight": down_weight, "down_first": down_first, "down_second": down_second, "norm_gains": norm_gains, "gains_first": gains_first, "gains_second": gains_second}


EPSILON = 1e-05
ROPE_BASE = 130000.0
BETA_ONE = 0.9
BETA_TWO = 0.95
ADAM_EPSILON = 1e-08
WEIGHT_DECAY = 0.1
GAIN_RATE = 0.5
MASK_VALUE = -1e+30
HIGHEST = lax.Precision.HIGHEST

@jax.custom_vjp
def low(v):
    return lax.optimization_barrier(v.astype(jnp.bfloat16)).astype(jnp.float32)

@jax.custom_vjp
def low_back(v):
    return v

def low_keep(v):
    return (low(v), None)

def low_pass(kept, grad):
    return (grad,)

def back_keep(v):
    return (v, None)

def back_low(kept, grad):
    return (low(grad),)
low.defvjp(low_keep, low_pass)
low_back.defvjp(back_keep, back_low)

def rms_norm(values, gain):
    return values * lax.rsqrt(lax.optimization_barrier(jnp.mean(values * values, axis=-1, keepdims=True)) + EPSILON) * gain

def rotary_tables(starts):
    places = (jnp.arange(starts.shape[0], dtype=jnp.int32) - starts).astype(jnp.float32)
    powers = jnp.arange(HEAD_DIM // 2, dtype=jnp.float32) * (2.0 / HEAD_DIM)
    angles = places[:, None] * (ROPE_BASE ** (-powers))[None, :]
    return (jnp.cos(angles)[:, None, :], jnp.sin(angles)[:, None, :])

def rotate(tensor, cosine, sine):
    half = tensor.shape[-1] // 2
    lower = tensor[..., :half]
    upper = tensor[..., half:]
    return jnp.concatenate([lower * cosine - upper * sine, upper * cosine + lower * sine], axis=-1)

def attend_block(query, query_starts, query_index, keys, values, starts):
    raw = low_back(jnp.einsum('qhd,khd->hqk', query, keys, precision=HIGHEST))
    key_index = jnp.arange(keys.shape[0], dtype=jnp.int32)
    allowed = (query_starts[:, None] == starts[None, :]) & (key_index[None, :] <= query_index[:, None])
    scores = jnp.where(allowed[None], raw * HEAD_DIM ** (-0.5), MASK_VALUE)
    probs = low(jax.nn.softmax(scores, axis=-1))
    return jnp.einsum('hqk,khd->qhd', probs, values, precision=HIGHEST)

def layer(resid, params, starts):
    in_w, out_w, up_w, down_w, gain_w = params
    count = resid.shape[0]
    cosine, sine = rotary_tables(starts)
    gains_low = low(gain_w)
    h_one = low(rms_norm(resid, gains_low[0]))
    projected = low_back(jnp.dot(h_one, low(in_w).reshape(D, 3 * D), precision=HIGHEST))
    projected = projected.reshape(count, 3, HEADS, HEAD_DIM)
    query = low(rotate(projected[:, 0], cosine, sine))
    keys = low(rotate(projected[:, 1], cosine, sine))
    values = low(projected[:, 2])
    block_rows = min(512, count)
    blocks = count // block_rows
    index = jnp.arange(count, dtype=jnp.int32)
    attend = jax.checkpoint(attend_block)
    heads_out = lax.map(lambda item: attend(item[0], item[1], item[2], keys, values, starts), (query.reshape(blocks, block_rows, HEADS, HEAD_DIM), starts.reshape(blocks, block_rows), index.reshape(blocks, block_rows)))
    attended = low(low_back(heads_out.reshape(count, D)))
    branch = low_back(jnp.dot(attended, low(out_w), precision=HIGHEST))
    hidden_in = resid + branch
    h_two = low(rms_norm(hidden_in, gains_low[1]))
    both = low_back(jnp.dot(h_two, low(up_w).reshape(D, 2 * FF), precision=HIGHEST)).reshape(count, 2, FF)
    inner = low(jax.nn.silu(both[:, 0]) * both[:, 1])
    return hidden_in + jnp.dot(inner, low(down_w), precision=HIGHEST)

def adam_step(weight, first_moment, second_moment, grad, rate, decay):
    new_first = BETA_ONE * first_moment + (1.0 - BETA_ONE) * grad
    new_second = BETA_TWO * second_moment + (1.0 - BETA_TWO) * grad * grad
    mean_part = new_first / (1.0 - BETA_ONE ** STEP)
    size_part = jnp.sqrt(new_second / (1.0 - BETA_TWO ** STEP)) + ADAM_EPSILON
    new_weight = weight - rate * (mean_part / size_part + decay * weight)
    return (new_first, new_second, new_weight)

def reference(tokens, cotangent, doc_start, in_weight, in_first, in_second, out_weight, out_first, out_second, gate_up, gate_up_first, gate_up_second, down_weight, down_first, down_second, norm_gains, gains_first, gains_second):
    weights = (in_weight, out_weight, gate_up, down_weight, norm_gains)
    inputs = tokens.astype(jnp.float32).reshape(N_DP, TOK_DEV, D)
    backs = cotangent.astype(jnp.float32).reshape(N_DP, TOK_DEV, D)
    starts = doc_start.reshape(N_DP, TOK_DEV)

    def group(totals, item):
        resid, back, start_slots = item

        def forward(resid_in, *params):
            return layer(resid_in, params, start_slots)
        result, pull = jax.vjp(forward, resid, *weights)
        grads = pull(back)
        totals = tuple((total + grad for total, grad in zip(totals, grads[1:])))
        return (totals, (result.astype(jnp.bfloat16), grads[0]))
    zeros = tuple((jnp.zeros(weight.shape, jnp.float32) for weight in weights))
    totals, (results, input_grads) = lax.scan(group, zeros, (inputs, backs, starts))
    in_grad, out_grad, up_grad, down_grad, gain_grad = totals
    in_new = adam_step(in_weight, in_first, in_second, in_grad, 2.0 * D ** (-0.5), WEIGHT_DECAY)
    out_new = adam_step(out_weight, out_first, out_second, out_grad, 2.0 * (D // 8) ** (-0.5), WEIGHT_DECAY)
    up_new = adam_step(gate_up, gate_up_first, gate_up_second, up_grad, 2.0 * D ** (-0.5), WEIGHT_DECAY)
    down_new = adam_step(down_weight, down_first, down_second, down_grad, 2.0 * FF ** (-0.5), WEIGHT_DECAY)
    gain_new = adam_step(norm_gains, gains_first, gains_second, gain_grad, GAIN_RATE, 0.0)
    return (results.reshape(TOKENS, D), input_grads.reshape(TOKENS, D), in_new[0], in_new[1], in_new[2], out_new[0], out_new[1], out_new[2], up_new[0], up_new[1], up_new[2], down_new[0], down_new[1], down_new[2], gain_new[0], gain_new[1], gain_new[2])
```

```python
import functools

import jax
import jax.numpy as jnp
from jax import lax
from jax.experimental.layout import Layout, with_layout_constraint
from jax.experimental import pallas as pl
from jax.experimental.pallas import tpu as pltpu
from jax.sharding import PartitionSpec as P

D = 2048
HEAD_DIM = 64
FF = 8192
STEP = 5


EPSILON = 1e-05
ROPE_BASE = 130000.0
BETA_ONE = 0.9
BETA_TWO = 0.95
ADAM_EPSILON = 1e-08
WEIGHT_DECAY = 0.1
GAIN_RATE = 0.5
MASK_VALUE = -1e30

MESH = pl.DeviceIdType.MESH
BF = jnp.bfloat16
F32 = jnp.float32
TILE = 256
LANES = 128
CHUNKS = 2
FINE = 4
FIRST = 4
VMEM_LIMIT = 60 * 1024 * 1024

WHOLE = pl.BlockSpec(memory_space=pltpu.VMEM)
ANY = pl.BlockSpec(memory_space=pl.ANY)


def nn(a, b):
    return lax.dot_general(a, b, (((1,), (0,)), ((), ())), preferred_element_type=F32)


def nt(a, b):
    return lax.dot_general(a, b, (((1,), (1,)), ((), ())), preferred_element_type=F32)


def tn(a, b):
    return lax.dot_general(a, b, (((0,), (0,)), ((), ())), preferred_element_type=F32)


def params(collective_id=None):
    if collective_id is None:
        return pltpu.CompilerParams(vmem_limit_bytes=VMEM_LIMIT)
    return pltpu.CompilerParams(
        vmem_limit_bytes=VMEM_LIMIT, collective_id=collective_id, has_side_effects=True
    )


def cost(microseconds):
    return pl.CostEstimate(
        flops=int(microseconds * 1.0e9), bytes_accessed=int(microseconds * 2.0e6), transcendentals=0
    )


def neighbours(me, n):
    return (me > 0).astype(jnp.int32) + (me < n - 1).astype(jnp.int32)


def chain_barrier(me, n):
    barrier = pltpu.get_barrier_semaphore()
    for there, other in ((me > 0, me - 1), (me < n - 1, me + 1)):

        @pl.when(there)
        def _(other=other):
            pl.semaphore_signal(barrier, inc=1, device_id={"tensor": other}, device_id_type=MESH)

    pl.semaphore_wait(barrier, neighbours(me, n))


def chips_barrier(me, n, line, m):
    chips = m // 2
    chip, core = line // 2, lax.rem(line, 2)
    barrier = pltpu.get_barrier_semaphore()
    for there, other in ((me > 0, me - 1), (me < n - 1, me + 1)):

        @pl.when(there)
        def _(other=other):
            pl.semaphore_signal(barrier, inc=1, device_id={"tensor": other}, device_id_type=MESH)

    pl.semaphore_signal(barrier, inc=1, device_id={"dp": 2 * chip + 1 - core}, device_id_type=MESH)
    for hop in range(1, chips):
        to = 2 * lax.rem(chip + hop, chips) + core
        pl.semaphore_signal(barrier, inc=1, device_id={"dp": to}, device_id_type=MESH)
    pl.semaphore_wait(barrier, neighbours(me, n) + chips)


def everyone_barrier(me, n, line, m):
    barrier = pltpu.get_barrier_semaphore()
    for hop in range(1, n):
        to = lax.rem(me + hop, n)
        pl.semaphore_signal(barrier, inc=1, device_id={"tensor": to}, device_id_type=MESH)
    for hop in range(1, m):
        to = lax.rem(line + hop, m)
        pl.semaphore_signal(barrier, inc=1, device_id={"dp": to}, device_id_type=MESH)
    pl.semaphore_wait(barrier, n + m - 2)


class Gather:
    def __init__(self, me, n, own, place, send, recv, chunks):
        self.me, self.n, self.own, self.place = me, n, own, place
        self.send, self.recv, self.chunks = send, recv, chunks

    def link(self, way, step, c):
        shard = self.me - step if way == 0 else self.me + step
        to = self.me + 1 if way == 0 else self.me - 1
        dst = self.place(shard, c)
        return pltpu.make_async_remote_copy(
            src_ref=self.own(c) if step == 0 else dst,
            dst_ref=dst,
            send_sem=self.send.at[way, step, c],
            recv_sem=self.recv.at[way, step, c],
            device_id={"tensor": to},
            device_id_type=MESH,
        )

    def holds(self, way, step):
        return self.me - step >= 0 if way == 0 else self.me + step <= self.n - 1

    def passes(self, way):
        return self.me < self.n - 1 if way == 0 else self.me > 0

    def start(self):
        for c in range(self.chunks):
            for way in range(2):

                @pl.when(self.passes(way))
                def _(way=way, c=c):
                    self.link(way, 0, c).start()

    def advance(self, step, only=None):
        for c in range(self.chunks) if only is None else (only,):
            for way in range(2):

                @pl.when(self.holds(way, step))
                def _(way=way, c=c):
                    shard = self.me - step if way == 0 else self.me + step
                    here = self.place(shard, c)
                    pltpu.make_async_remote_copy(
                        src_ref=here,
                        dst_ref=here,
                        send_sem=self.send.at[way, step - 1, c],
                        recv_sem=self.recv.at[way, step - 1, c],
                        device_id={"tensor": self.me},
                        device_id_type=MESH,
                    ).wait_recv()
                    if step < self.n - 1:

                        @pl.when(self.passes(way))
                        def _():
                            self.link(way, step, c).start()

    def finish(self):
        for step in range(self.n - 1):
            for c in range(self.chunks):
                for way in range(2):

                    @pl.when(self.holds(way, step) & self.passes(way))
                    def _(way=way, c=c, step=step):
                        self.link(way, step, c).wait_send()


def gather_sems(n, chunks):
    return [pltpu.SemaphoreType.DMA((2, n - 1, chunks)), pltpu.SemaphoreType.DMA((2, n - 1, chunks))]


def nth_dest(me, n, i):
    if i == n - 1:
        return me
    both = jnp.minimum(me, n - 1 - me)
    near = jnp.where((me < n // 2) == (i % 2 == 0), n - 1 - i // 2, i // 2)
    late = i - both
    return jnp.where(i < 2 * both, near, jnp.where(n - 1 - me > me, n - 1 - late, late))


class Scatter:
    def __init__(self, me, n, part, own, inbox, send, recv, chunks):
        self.me, self.n, self.part, self.own, self.inbox = me, n, part, own, inbox
        self.send, self.recv, self.chunks = send, recv, chunks
        self.size = part.shape[1] // chunks
        self.events = (n - 1) * chunks + n - 2

    def rows(self, c):
        return pl.ds(pl.multiple_of(c * self.size, self.size), self.size)

    def box(self, way, step, c):
        return self.inbox.at[step if way == 0 else self.n - step, self.rows(c)]

    def hop(self, way, dest, c):
        step = self.n - 1 - dest if way == 0 else dest
        return pltpu.make_async_remote_copy(
            src_ref=self.part.at[dest, self.rows(c)],
            dst_ref=self.box(way, step, c),
            send_sem=self.send.at[way, step, c],
            recv_sem=self.recv.at[way, step, c],
            device_id={"tensor": self.me + 1 if way == 0 else self.me - 1},
            device_id_type=MESH,
        )

    def offer(self, dest):
        for way in range(2):
            first = (self.me == 0) & (dest > self.me) if way == 0 else (self.me == self.n - 1) & (dest < self.me)

            @pl.when(first)
            def _(way=way):
                for c in range(self.chunks):
                    self.hop(way, dest, c).start()

    def relay(self, time):
        for way in range(2):
            number = time - (self.me - 1) if way == 0 else time - (self.n - 2 - self.me)
            inside = (number >= 0) & (number < (self.n - 1) * self.chunks)
            number = jnp.where(inside, number, 0)
            step = number // self.chunks
            c = number - step * self.chunks
            dest = self.n - 1 - step if way == 0 else step
            if way == 0:
                live = inside & (self.me > 0) & (dest >= self.me)
            else:
                live = inside & (self.me < self.n - 1) & (dest <= self.me)

            @pl.when(live)
            def _(way=way, step=step, c=c, dest=dest):
                here = self.box(way, step, c)
                pltpu.make_async_remote_copy(
                    src_ref=here,
                    dst_ref=here,
                    send_sem=self.send.at[way, step, c],
                    recv_sem=self.recv.at[way, step, c],
                    device_id={"tensor": self.me},
                    device_id_type=MESH,
                ).wait_recv()
                rows = self.rows(c)

                @pl.when(dest == self.me)
                def _():
                    self.own[rows] = self.own[rows] + here[...].astype(F32)

                @pl.when(dest != self.me)
                def _():
                    self.part[dest, rows] = self.part[dest, rows] + here[...]
                    self.hop(way, dest, c).start()

    def relays(self, first, last):
        def body(time, carry):
            self.relay(time)
            return carry

        lax.fori_loop(first, last, body, 0)

    def finish(self):
        for step in range(self.n - 1):
            for c in range(self.chunks):
                for way in range(2):
                    dest = self.n - 1 - step if way == 0 else step

                    @pl.when(self.me < dest if way == 0 else self.me > dest)
                    def _(way=way, dest=dest, c=c):
                        self.hop(way, dest, c).wait_send()


def scatter_scratch(n, rows, width, chunks):
    return [
        pltpu.VMEM((n, rows, width), BF),
        pltpu.VMEM((n + 1, rows, width), BF),
        pltpu.SemaphoreType.DMA((2, n - 1, chunks)),
        pltpu.SemaphoreType.DMA((2, n - 1, chunks)),
    ]


class ChipScatter:
    def __init__(self, line, m, mine, theirs, half, box, pair_send, pair_recv, chip_send, chip_recv):
        self.chips = m // 2
        self.square = self.chips == 4
        self.chip, self.core = line // 2, lax.rem(line, 2)
        self.mine, self.theirs, self.half, self.box = mine, theirs, half, box
        self.pair_send, self.pair_recv = pair_send, pair_recv
        self.chip_send, self.chip_recv = chip_send, chip_recv
        self.kinds, self.size = mine.shape[1], mine.shape[2]
        order = [3, 1, 2, 0] if self.square else list(range(1, self.chips)) + [0]
        self.steps = [(hop, other) for hop in order for other in (True, False)]

    def device(self, hop, core):
        if self.square:
            x, y = lax.rem(self.chip, 2), self.chip // 2
            return 2 * (2 * lax.rem(y + hop // 2, 2) + lax.rem(x + hop % 2, 2)) + core
        return 2 * lax.rem(self.chip + hop, self.chips) + core

    def target(self, at):
        hop, other = self.steps[at]
        return self.device(hop, 1 - self.core if other else self.core)

    def slot(self, at):
        hop, other = self.steps[at]
        return self.theirs.at[hop] if other else self.mine.at[hop]

    def to_pair(self, hop):
        return pltpu.make_async_remote_copy(
            src_ref=self.theirs.at[hop],
            dst_ref=self.half.at[hop],
            send_sem=self.pair_send.at[hop],
            recv_sem=self.pair_recv.at[hop],
            device_id={"dp": 2 * self.chip + 1 - self.core},
            device_id_type=MESH,
        )

    def to_chip(self, hop):
        return pltpu.make_async_remote_copy(
            src_ref=self.mine.at[hop],
            dst_ref=self.box.at[hop],
            send_sem=self.chip_send.at[hop],
            recv_sem=self.chip_recv.at[hop],
            device_id={"dp": self.device(hop, self.core)},
            device_id_type=MESH,
        )

    def over(self, hop):
        rows = pl.ds((hop - 1) * self.size // 2, self.size // 2)
        sem = 3 if hop == 1 else 0
        return pltpu.make_async_remote_copy(
            src_ref=self.mine.at[3, :, rows],
            dst_ref=self.box.at[3, :, rows],
            send_sem=self.chip_send.at[sem],
            recv_sem=self.chip_recv.at[sem],
            device_id={"dp": self.device(hop, self.core)},
            device_id_type=MESH,
        )

    def filled(self, at):
        hop, other = self.steps[at]
        if other:
            self.to_pair(hop).start()
            if at >= 2:
                self.combine(self.steps[at - 1][0])

    def combine(self, hop):
        self.to_pair(hop).wait_recv()
        for kind in range(self.kinds):
            self.mine[hop, kind] = self.mine[hop, kind] + self.half[hop, kind]
        if not self.square:
            if hop > 0:
                self.to_chip(hop).start()
        elif hop == 3:
            self.over(1).start()
            self.over(2).start()

    def forward(self):
        if not self.square:
            return
        for via, hop in ((1, 2), (2, 1)):
            self.over(via).wait_recv()
            rows = pl.ds((via - 1) * self.size // 2, self.size // 2)
            for kind in range(self.kinds):
                self.mine[hop, kind, rows] = self.mine[hop, kind, rows] + self.box[3, kind, rows]
            self.to_chip(hop).start()

    def final(self):
        return (1, 2) if self.square else tuple(range(1, self.chips))

    def arrive(self):
        for hop in self.final():
            self.to_chip(hop).wait_recv()

    def result(self, kind):
        total = self.mine[0, kind].astype(F32)
        for hop in self.final():
            total = total + self.box[hop, kind].astype(F32)
        return total

    def finish(self):
        for hop in range(self.chips):
            self.to_pair(hop).wait_send()
        for hop in self.final():
            self.to_chip(hop).wait_send()
        if self.square:
            self.over(1).wait_send()
            self.over(2).wait_send()


def chip_scatter_scratch(m, shard):
    return [pltpu.VMEM((m // 2,) + shard, BF)] * 4 + [pltpu.SemaphoreType.DMA((m // 2,))] * 4


def half_swap(values):
    lane = lax.broadcasted_iota(jnp.int32, values.shape, 1)
    lower = lax.rem(lane, HEAD_DIM) < HEAD_DIM // 2
    return jnp.where(
        lower, pltpu.roll(values, LANES - HEAD_DIM // 2, 1), pltpu.roll(values, HEAD_DIM // 2, 1)
    )


def row_scale(values):
    return lax.rsqrt(jnp.mean(values * values, axis=-1, keepdims=True) + EPSILON)


def first_kernel(n, m, out_ref, gain_ref, all_out, all_gain, send, recv, gain_send, gain_recv, local_sem):
    me = lax.axis_index("tensor")
    line = lax.axis_index("dp")
    barrier = pltpu.get_barrier_semaphore()
    for hop in range(1, m):
        pl.semaphore_signal(
            barrier, inc=1, device_id={"dp": lax.rem(line + hop, m)}, device_id_type=MESH
        )
    for there, other in ((me > 0, me - 1), (me < n - 1, me + 1)):

        @pl.when(there)
        def _(other=other):
            pl.semaphore_signal(barrier, inc=1, device_id={"tensor": other}, device_id_type=MESH)

    pl.semaphore_wait(barrier, m - 1 + neighbours(me, n))

    size = out_ref.shape[0] // CHUNKS
    gather = Gather(
        me,
        n,
        lambda c: out_ref.at[pl.ds(c * size, size)],
        lambda shard, c: all_out.at[shard, pl.ds(c * size, size)],
        send,
        recv,
        CHUNKS,
    )
    gather.start()

    def gain_copy(hop):
        return pltpu.make_async_remote_copy(
            src_ref=gain_ref,
            dst_ref=all_gain.at[line],
            send_sem=gain_send.at[hop],
            recv_sem=gain_recv.at[hop],
            device_id={"dp": lax.rem(line + hop, m)},
            device_id_type=MESH,
        )

    for hop in range(1, m):
        gain_copy(hop).start()
    mine = pltpu.make_async_copy(out_ref, all_out.at[me], local_sem.at[0])
    mine.start()
    mine_gain = pltpu.make_async_copy(gain_ref, all_gain.at[line], local_sem.at[1])
    mine_gain.start()
    for step in range(1, n):
        gather.advance(step)
    for hop in range(1, m):
        source = lax.rem(line + m - hop, m)
        pltpu.make_async_remote_copy(
            src_ref=gain_ref,
            dst_ref=all_gain.at[source],
            send_sem=gain_send.at[hop],
            recv_sem=gain_recv.at[hop],
            device_id={"dp": source},
            device_id_type=MESH,
        ).wait_recv()
    for hop in range(1, m):
        gain_copy(hop).wait_send()
    gather.finish()
    mine.wait()
    mine_gain.wait()


def gather_first(n, m, out_low, gains):
    rows, width = out_low.shape
    return pl.pallas_call(
        functools.partial(first_kernel, n, m),
        name="gather_out_shards",
        out_shape=(
            jax.ShapeDtypeStruct((n, rows, width), BF),
            jax.ShapeDtypeStruct((m,) + gains.shape, F32),
        ),
        in_specs=[ANY, ANY],
        out_specs=(ANY, ANY),
        scratch_shapes=gather_sems(n, CHUNKS)
        + [
            pltpu.SemaphoreType.DMA((m,)),
            pltpu.SemaphoreType.DMA((m,)),
            pltpu.SemaphoreType.DMA((2,)),
        ],
        compiler_params=params(0),
        cost_estimate=cost(20),
    )(out_low, gains)


def rows_kernel(
    n,
    x_ref,
    up_hbm,
    down_hbm,
    start_ref,
    freq_ref,
    all_x,
    low_ref,
    cos_ref,
    sin_ref,
    send,
    recv,
    up,
    down,
    local_sem,
    load_sem,
):
    me = lax.axis_index("tensor")
    size = x_ref.shape[0] // CHUNKS
    loads = (
        pltpu.make_async_copy(up_hbm, up, load_sem.at[0]),
        pltpu.make_async_copy(down_hbm, down, load_sem.at[1]),
    )
    for copy in loads:
        copy.start()
    chain_barrier(me, n)
    gather = Gather(
        me,
        n,
        lambda c: x_ref.at[pl.ds(c * size, size)],
        lambda shard, c: all_x.at[shard, pl.ds(c * size, size)],
        send,
        recv,
        CHUNKS,
    )
    gather.start()
    mine = pltpu.make_async_copy(x_ref, all_x.at[me], local_sem)
    mine.start()
    for copy in loads:
        copy.wait()
    hidden, each = down.shape

    def cast(r, carry):
        rows = pl.ds(pl.multiple_of(r * 32, 32), 32)
        for kind in range(2):
            low_ref[kind, rows] = up[rows, kind, :].astype(BF)
        return carry

    lax.fori_loop(0, each // 32, cast, 0)

    def turn(c, carry):
        cols = pl.ds(pl.multiple_of(c * TILE, TILE), TILE)
        low_ref[2, :, cols] = jnp.transpose(down[cols]).astype(BF)
        return carry

    lax.fori_loop(0, hidden // TILE, turn, 0)
    gather.advance(1)

    def table(r, carry):
        rows = pl.ds(pl.multiple_of(r * 64, 64), 64)
        place = lax.broadcasted_iota(jnp.int32, (64, LANES), 0) + r * 64 - start_ref[rows]
        lane = lax.broadcasted_iota(jnp.int32, (64, LANES), 1)
        angle = place.astype(F32) * freq_ref[0:1]
        cos_ref[rows] = jnp.cos(angle)
        sine = jnp.sin(angle)
        sin_ref[rows] = jnp.where(lax.rem(lane, HEAD_DIM) < HEAD_DIM // 2, -sine, sine)
        return carry

    lax.fori_loop(0, cos_ref.shape[0] // 64, table, 0)
    for step in range(2, n):
        gather.advance(step)
    gather.finish()
    mine.wait()


def gather_rows(n, x, gate_up, down_weight, starts, freqs):
    each, _, hidden = gate_up.shape
    table = jax.ShapeDtypeStruct(starts.shape, F32)
    return pl.pallas_call(
        functools.partial(rows_kernel, n),
        name="gather_tokens",
        out_shape=(
            jax.ShapeDtypeStruct((n,) + x.shape, BF),
            jax.ShapeDtypeStruct((3, each, hidden), BF),
            table,
            table,
        ),
        in_specs=[ANY] * 3 + [WHOLE] * 2,
        out_specs=(ANY, WHOLE, WHOLE, WHOLE),
        scratch_shapes=gather_sems(n, CHUNKS)
        + [
            pltpu.VMEM(gate_up.shape, F32),
            pltpu.VMEM(down_weight.shape, F32),
            pltpu.SemaphoreType.DMA,
            pltpu.SemaphoreType.DMA((2,)),
        ],
        compiler_params=params(1),
        cost_estimate=cost(65),
    )(x, gate_up, down_weight, starts, freqs)


def attend_kernel(
    n,
    x_hbm,
    gain_ref,
    w_hbm,
    cos_ref,
    sin_ref,
    start_ref,
    back_ref,
    h_hbm,
    qkv_hbm,
    att_hbm,
    lse_ref,
    scale_ref,
    all_back,
    send,
    recv,
    local_sem,
    x_ref,
    w_ref,
    h_ref,
    qkv_ref,
    att_ref,
    move_sem,
):
    me = lax.axis_index("tensor")
    count = x_ref.shape[0]
    width = w_ref.shape[2]
    blocks = count // TILE
    moves = [
        pltpu.make_async_copy(src, dst, move_sem.at[at])
        for at, (src, dst) in enumerate(
            ((x_hbm, x_ref), (w_hbm, w_ref), (h_ref, h_hbm), (qkv_ref, qkv_hbm), (att_ref, att_hbm))
        )
    ]
    moves[0].start()
    moves[1].start()
    size = back_ref.shape[0] // CHUNKS
    chain_barrier(me, n)
    gather = Gather(
        me,
        n,
        lambda c: back_ref.at[pl.ds(c * size, size)],
        lambda shard, c: all_back.at[shard, pl.ds(c * size, size)],
        send,
        recv,
        CHUNKS,
    )
    gather.start()
    mine = pltpu.make_async_copy(back_ref, all_back.at[me], local_sem)
    mine.start()

    def project(r, carry):
        rows = pl.ds(pl.multiple_of(r * TILE, TILE), TILE)
        x = x_ref[rows].astype(F32)
        scale = row_scale(x)
        scale_ref[rows] = jnp.broadcast_to(scale, (TILE, LANES))
        h = (x * scale * gain_ref[0:1]).astype(BF)
        h_ref[rows] = h
        cosine, sine = cos_ref[rows], sin_ref[rows]
        for kind in range(3):
            value = nn(h, w_ref[kind])
            if kind < 2:
                value = jnp.concatenate(
                    [
                        value[:, c : c + LANES] * cosine + half_swap(value[:, c : c + LANES]) * sine
                        for c in range(0, width, LANES)
                    ],
                    axis=1,
                )
            qkv_ref[kind, rows] = value.astype(BF)
        return carry

    moves[0].wait()
    moves[1].wait()
    lax.fori_loop(0, blocks, project, 0)
    moves[2].start()
    moves[3].start()

    lane = lax.broadcasted_iota(jnp.int32, (TILE, LANES), 1)
    key_lane = lax.broadcasted_iota(jnp.int32, (TILE, TILE), 1)
    query_row = lax.broadcasted_iota(jnp.int32, (TILE, TILE), 0)
    diagonal = key_lane <= query_row

    def pair(p, carry):
        cols = pl.ds(pl.multiple_of(p * LANES, LANES), LANES)
        for i in range(blocks):
            rows = pl.ds(i * TILE, TILE)
            query = qkv_ref[0, rows, cols] * jnp.asarray(HEAD_DIM ** (-0.5), BF)
            begin = start_ref[rows, 0:1]
            result = jnp.zeros((TILE, LANES), F32)
            for e in range(2):
                ours = lane < HEAD_DIM if e == 0 else lane >= HEAD_DIM
                q = jnp.where(ours, query, jnp.zeros_like(query))
                scores = []
                for j in range(i + 1):
                    s = nt(q, qkv_ref[1, pl.ds(j * TILE, TILE), cols])
                    allowed = key_lane >= begin - j * TILE
                    if j == i:
                        allowed = allowed & diagonal
                    scores.append(jnp.where(allowed, s, MASK_VALUE))
                top = functools.reduce(jnp.maximum, scores)
                peak = jnp.max(top, axis=-1, keepdims=True)
                expo = [jnp.exp(s - peak) for s in scores]
                total = jnp.sum(functools.reduce(jnp.add, expo), axis=-1, keepdims=True)
                acc = jnp.zeros((TILE, LANES), F32)
                for j in range(i + 1):
                    v = qkv_ref[2, pl.ds(j * TILE, TILE), cols]
                    acc = acc + nn(expo[j].astype(BF), jnp.where(ours, v, jnp.zeros_like(v)))
                result = result + acc / total
                lse = jnp.broadcast_to(peak + jnp.log(total), (TILE, LANES))
                lse_ref[pl.ds(2 * p + e, 1), rows] = jnp.transpose(lse)[0:1]
            att_ref[rows, cols] = result.astype(BF)
        return carry

    pairs = width // LANES
    lax.fori_loop(0, pairs // 2, pair, 0)
    gather.advance(1)
    lax.fori_loop(pairs // 2, pairs, pair, 0)
    moves[4].start()
    for step in range(2, n):
        gather.advance(step)
    gather.finish()
    mine.wait()
    for move in moves[2:]:
        move.wait()


def attend(n, x, gain, weights, cosine, sine, starts, back):
    count, depth = x.shape
    width = weights.shape[2]
    return pl.pallas_call(
        functools.partial(attend_kernel, n),
        name="attention_forward",
        out_shape=(
            jax.ShapeDtypeStruct((count, depth), BF),
            jax.ShapeDtypeStruct((3, count, width), BF),
            jax.ShapeDtypeStruct((count, width), BF),
            jax.ShapeDtypeStruct((width // HEAD_DIM, count), F32),
            jax.ShapeDtypeStruct((count, LANES), F32),
            jax.ShapeDtypeStruct((n,) + back.shape, BF),
        ),
        in_specs=[ANY, WHOLE, ANY, WHOLE, WHOLE, WHOLE, ANY],
        out_specs=(ANY, ANY, ANY, WHOLE, WHOLE, ANY),
        scratch_shapes=gather_sems(n, CHUNKS)
        + [
            pltpu.SemaphoreType.DMA,
            pltpu.VMEM((count, depth), BF),
            pltpu.VMEM(weights.shape, BF),
            pltpu.VMEM((count, depth), BF),
            pltpu.VMEM((3, count, width), BF),
            pltpu.VMEM((count, width), BF),
            pltpu.SemaphoreType.DMA((5,)),
        ],
        compiler_params=params(2),
        cost_estimate=cost(65),
    )(x, gain, weights, cosine, sine, starts, back)


def branch_kernel(
    n, att_ref, w_hbm, x_hbm, gain_ref, h_ref, hidden_ref, held, total, send, recv, w_ref, x_ref, load_sem
):
    me = lax.axis_index("tensor")
    count, width = att_ref.shape
    rows_each = hidden_ref.shape[0]
    size = count // CHUNKS
    loads = (
        pltpu.make_async_copy(w_hbm, w_ref, load_sem.at[0]),
        pltpu.make_async_copy(x_hbm, x_ref, load_sem.at[1]),
    )
    for copy in loads:
        copy.start()
    chain_barrier(me, n)
    gather = Gather(
        me,
        n,
        lambda c: att_ref.at[pl.ds(c * size, size)],
        lambda shard, c: held.at[shard, pl.ds(c * size, size)],
        send,
        recv,
        CHUNKS,
    )
    gather.start()

    def add(source, shard, first, start, stop):
        weights = pl.ds(pl.multiple_of(shard * width, width), width)

        def tile(r, carry):
            rows = pl.ds(pl.multiple_of(r * TILE, TILE), TILE)
            term = nn(source[rows], w_ref[weights])
            total[rows] = term + (x_ref[rows].astype(F32) if first else total[rows])
            return carry

        lax.fori_loop(start // TILE, stop // TILE, tile, 0)

    def arrived(step, start, stop):
        for way in range(2):

            @pl.when(gather.holds(way, step))
            def _(way=way):
                shard = me - step if way == 0 else me + step
                add(held.at[shard], shard, False, start, stop)

    def norm(r, carry):
        rows = pl.ds(pl.multiple_of(r * LANES, LANES), LANES)
        hidden = total[rows]
        h_ref[rows] = (hidden * row_scale(hidden) * gain_ref[1:2]).astype(BF)
        return carry

    for copy in loads:
        copy.wait()
    add(att_ref, me, True, 0, count)
    for step in range(1, n - 1):
        gather.advance(step)
        arrived(step, 0, count)
    for c in range(CHUNKS):
        gather.advance(n - 1, c)
        arrived(n - 1, c * size, (c + 1) * size)
        lax.fori_loop(c * size // LANES, (c + 1) * size // LANES, norm, 0)
    hidden_ref[...] = total[pl.ds(pl.multiple_of(me * rows_each, rows_each), rows_each)]
    gather.finish()


def project_branch(n, att, weights, x, gain):
    count, width = att.shape
    depth = x.shape[1]
    return pl.pallas_call(
        functools.partial(branch_kernel, n),
        name="branch",
        out_shape=(
            jax.ShapeDtypeStruct((count, depth), BF),
            jax.ShapeDtypeStruct((count // n, depth), F32),
        ),
        in_specs=[WHOLE, ANY, ANY, WHOLE],
        out_specs=(WHOLE, WHOLE),
        scratch_shapes=[pltpu.VMEM((n, count, width), BF), pltpu.VMEM((count, depth), F32)]
        + gather_sems(n, CHUNKS)
        + [
            pltpu.VMEM((depth, depth), BF),
            pltpu.VMEM(x.shape, BF),
            pltpu.SemaphoreType.DMA((2,)),
        ],
        compiler_params=params(3),
        cost_estimate=cost(70),
    )(att, weights, x, gain)


def feed_kernel(
    n,
    h_hbm,
    back_hbm,
    w_hbm,
    inner_hbm,
    both_hbm,
    own_ref,
    part,
    inbox,
    send,
    recv,
    w,
    inner_ref,
    both,
    h_rows,
    back_rows,
    w_sem,
    row_sem,
    store_sem,
):
    me = lax.axis_index("tensor")
    rows_each, depth = own_ref.shape
    hidden = inner_ref.shape[1]
    tiles = hidden // TILE
    pair = 2 if tiles % 2 == 0 else 1

    def fetch(b):
        cols = pl.ds(pl.multiple_of(b * TILE, TILE), TILE)
        return pltpu.make_async_copy(w_hbm.at[:, :, cols], w.at[:, :, cols], w_sem.at[b])

    def fetch_rows(dest):
        rows = pl.ds(pl.multiple_of(dest * rows_each, rows_each), rows_each)
        return (
            pltpu.make_async_copy(h_hbm.at[rows], h_rows, row_sem.at[0]),
            pltpu.make_async_copy(back_hbm.at[rows], back_rows, row_sem.at[1]),
        )

    def stores(i, dest):
        rows = pl.ds(pl.multiple_of(dest * rows_each, rows_each), rows_each)
        return (
            pltpu.make_async_copy(inner_ref.at[rows], inner_hbm.at[rows], store_sem.at[i, 0]),
            pltpu.make_async_copy(both.at[:, rows], both_hbm.at[:, rows], store_sem.at[i, 1]),
        )

    for copy in fetch_rows(nth_dest(me, n, 0)):
        copy.start()
    for b in range(tiles):
        fetch(b).start()
    chain_barrier(me, n)
    scatter = Scatter(me, n, part, own_ref, inbox, send, recv, FINE)
    own_ref[...] = jnp.zeros_like(own_ref)
    step_cols = 512
    steps = tiles // pair
    per_block = steps + depth // step_cols
    last = n * per_block
    due = [last + 1] * scatter.events
    if n == 4 and per_block == 8:
        due = [11, 16, 17, 19, 24, 25, 26, 28, 31] + due[9:]

    def serve(tick):
        def count(now):
            return functools.reduce(jnp.add, [(now >= at).astype(jnp.int32) for at in due])

        scatter.relays(count(tick - 1), count(tick))

    for i in range(n):
        dest = nth_dest(me, n, i)
        rows = pl.ds(pl.multiple_of(dest * rows_each, rows_each), rows_each)
        for copy in fetch_rows(dest):
            copy.wait()

        def forward(b, carry, i=i, rows=rows):
            if i == 0:
                for half in range(pair):
                    fetch(pair * b + half).wait()
            for half in range(pair):
                cols = pl.ds(pl.multiple_of((pair * b + half) * TILE, TILE), TILE)
                gate = nn(h_rows[...], w[0, :, cols])
                up = nn(h_rows[...], w[1, :, cols])
                d_inner = nn(back_rows[...], w[2, :, cols])
                sigmoid = jax.nn.sigmoid(gate)
                silu = gate * sigmoid
                inner_ref[rows, cols] = (silu * up).astype(BF)
                both[0, rows, cols] = (d_inner * up * sigmoid * (1.0 + gate * (1.0 - sigmoid))).astype(BF)
                both[1, rows, cols] = (d_inner * silu).astype(BF)
            if i > 0:
                serve(i * per_block + 1 + b)
            return carry

        lax.fori_loop(0, steps, forward, 0)
        if i < n - 1:
            for copy in fetch_rows(nth_dest(me, n, i + 1)):
                copy.start()
        for copy in stores(i, dest):
            copy.start()

        def backward(c, carry, i=i, rows=rows, dest=dest):
            cols = pl.ds(pl.multiple_of(c * step_cols, step_cols), step_cols)
            value = nt(both[0, rows], w[0, cols]) + nt(both[1, rows], w[1, cols])
            if i < n - 1:
                part[dest, :, cols] = value.astype(BF)
            else:
                own_ref[:, cols] = own_ref[:, cols] + value
            if i > 0:
                serve(i * per_block + steps + 1 + c)
            return carry

        lax.fori_loop(0, depth // step_cols, backward, 0)
        if i < n - 1:
            scatter.offer(dest)

    late = [at for at in range(scatter.events) if due[at] > last]
    scatter.relays(late[0], scatter.events)
    for i in range(n):
        for copy in stores(i, nth_dest(me, n, i)):
            copy.wait()
    scatter.finish()


def feed(n, h, back, weights):
    count, depth = h.shape
    hidden = weights.shape[2]
    rows = count // n
    return pl.pallas_call(
        functools.partial(feed_kernel, n),
        name="feed_forward",
        out_shape=(
            jax.ShapeDtypeStruct((count, hidden), BF),
            jax.ShapeDtypeStruct((2, count, hidden), BF),
            jax.ShapeDtypeStruct((rows, depth), F32),
        ),
        in_specs=[ANY] * 3,
        out_specs=(ANY, ANY, WHOLE),
        scratch_shapes=scatter_scratch(n, rows, depth, FINE)
        + [
            pltpu.VMEM((3, depth, hidden), BF),
            pltpu.VMEM((count, hidden), BF),
            pltpu.VMEM((2, count, hidden), BF),
            pltpu.VMEM((rows, depth), BF),
            pltpu.VMEM((rows, depth), BF),
            pltpu.SemaphoreType.DMA((hidden // TILE,)),
            pltpu.SemaphoreType.DMA((2,)),
            pltpu.SemaphoreType.DMA((n, 2)),
        ],
        compiler_params=params(4),
        cost_estimate=cost(95),
    )(h, back, weights)


def branch_back_kernel(
    n,
    m,
    d_two_ref,
    hidden_ref,
    cot_ref,
    gain_ref,
    w_hbm,
    h_hbm,
    both_hbm,
    back_hbm,
    inner_hbm,
    feed_hbm,
    d_hidden_ref,
    d_att_ref,
    gain_part_ref,
    all_hbm,
    grad_hbm,
    down_ref,
    first_ref,
    held,
    w_ref,
    send,
    recv,
    w_sem,
    out_sem,
    both,
    inner,
    h_cols,
    back_cols,
    slot,
    both_sem,
    col_sem,
    slot_sem,
    down,
    part,
    inbox,
    s_send,
    s_recv,
    *chip_scratch,
):
    me = lax.axis_index("tensor")
    line = lax.axis_index("dp")
    down_sum = ChipScatter(line, m, *chip_scratch)
    rows_each, depth = hidden_ref.shape
    width = d_att_ref.shape[1]
    size = rows_each // CHUNKS
    fetch = pltpu.make_async_copy(
        w_hbm.at[pl.ds(pl.multiple_of(me * width, width), width)], w_ref, w_sem
    )
    fetch.start()
    loads = (
        pltpu.make_async_copy(inner_hbm, inner, both_sem.at[0]),
        pltpu.make_async_copy(feed_hbm.at[2, pl.ds(0, down.shape[0])], down, both_sem.at[1]),
        pltpu.make_async_copy(both_hbm, both, both_sem.at[2]),
    )
    for copy in loads:
        copy.start()
    each = depth // m

    def fetch_cols(at):
        cols = pl.ds(pl.multiple_of(at * each, each), each)
        to = lax.rem(at, 2)
        return pltpu.make_async_copy(h_hbm.at[:, cols], h_cols.at[to], col_sem.at[0, to])

    def fetch_back(at):
        cols = pl.ds(pl.multiple_of(down_sum.target(at) * each, each), each)
        return pltpu.make_async_copy(back_hbm.at[:, cols], back_cols.at[at % 2], col_sem.at[1, at % 2])

    fetch_cols(0).start()
    fetch_back(0).start()
    chips_barrier(me, n, line, m)
    step_rows = min(LANES, rows_each)
    gain_part_ref[...] = jnp.zeros_like(gain_part_ref)

    def norm(r, carry):
        rows = pl.ds(pl.multiple_of(r * step_rows, step_rows), step_rows)
        hidden = hidden_ref[rows]
        scale = row_scale(hidden)
        normed = hidden * scale
        d_two = d_two_ref[rows]
        scaled = d_two * gain_ref[1:2]
        back = scale * (scaled - normed * jnp.mean(scaled * normed, axis=-1, keepdims=True))
        d_hidden = cot_ref[rows].astype(F32) + back
        d_hidden_ref[rows] = d_hidden
        held[me, rows] = d_hidden.astype(BF)
        gain_part_ref[1:2] = gain_part_ref[1:2] + jnp.sum(d_two * normed, axis=0, keepdims=True)
        return carry

    lax.fori_loop(0, rows_each // step_rows, norm, 0)

    gather = Gather(
        me,
        n,
        lambda c: held.at[me, pl.ds(c * size, size)],
        lambda shard, c: held.at[shard, pl.ds(c * size, size)],
        send,
        recv,
        CHUNKS,
    )
    gather.start()

    def use(shard):
        rows = pl.ds(pl.multiple_of(shard * rows_each, rows_each), rows_each)
        pltpu.make_async_copy(held.at[shard], all_hbm.at[shard], out_sem.at[shard]).start()
        d_att_ref[rows] = nt(held[shard], w_ref[...]).astype(BF)

    def out_copy(at, kind):
        return pltpu.make_async_copy(slot.at[kind], grad_hbm.at[2 * at + kind], slot_sem.at[kind])

    step_cols = 512
    tiles = inner.shape[1] // step_cols

    def up_piece(at, carry):
        @pl.when(at + 1 < m)
        def _():
            fetch_cols(at + 1).start()

        fetch_cols(at).wait()
        turned = jnp.transpose(h_cols[lax.rem(at, 2)])
        for kind in range(2):

            @pl.when(at > 0)
            def _(kind=kind):
                out_copy(at - 1, kind).wait()

            def tile(c, inner_carry, kind=kind):
                cols = pl.ds(pl.multiple_of(c * step_cols, step_cols), step_cols)
                slot[kind, :, cols] = nn(turned, both[kind, :, cols]).astype(BF)
                return inner_carry

            lax.fori_loop(0, tiles, tile, 0)
            out_copy(at, kind).start()
        return carry

    def down_piece(at):
        if at + 1 < m:
            fetch_back(at + 1).start()
        fetch_back(at).wait()
        turned = jnp.transpose(back_cols[at % 2])
        to = down_sum.slot(at)

        def tile(c, carry):
            cols = pl.ds(pl.multiple_of(c * step_cols, step_cols), step_cols)
            to[0, :, cols] = nn(turned, inner[:, cols]).astype(BF)
            return carry

        lax.fori_loop(0, tiles, tile, 0)
        down_sum.filled(at)

    scatter = Scatter(me, n, part, first_ref, inbox, s_send, s_recv, CHUNKS)
    first_ref[...] = hidden_ref[:, 0 : first_ref.shape[1]]
    loads[0].wait()
    loads[1].wait()
    for i in range(n):
        dest = nth_dest(me, n, i)
        rows = pl.ds(pl.multiple_of(dest * rows_each, rows_each), rows_each)
        value = nt(inner[rows], down[...])
        if i < n - 1:
            part[dest] = value.astype(BF)
            scatter.offer(dest)
        else:
            first_ref[...] = first_ref[...] + value
    for at in range(m):
        down_piece(at)
    fetch.wait()
    use(me)
    down_sum.combine(0)
    down_sum.forward()
    loads[2].wait()

    def arrived(step):
        for way in range(2):

            @pl.when(gather.holds(way, step))
            def _(way=way):
                use(me - step if way == 0 else me + step)

    gather.advance(1)
    arrived(1)
    lax.fori_loop(0, m // 2, up_piece, 0)
    gather.advance(2)
    arrived(2)
    lax.fori_loop(m // 2, m, up_piece, 0)
    scatter.relays(0, scatter.events)
    down_sum.arrive()
    down_ref[...] = jnp.transpose(down_sum.result(0))
    for step in range(3, n):
        gather.advance(step)
        arrived(step)
    for kind in range(2):
        out_copy(m - 1, kind).wait()
    for shard in range(n):
        pltpu.make_async_copy(held.at[shard], all_hbm.at[shard], out_sem.at[shard]).wait()
    gather.finish()
    scatter.finish()
    down_sum.finish()


def branch_back(n, m, d_two, hidden, cotangent, gain, out_weights, h, both, back, inner, feed_weights, width):
    rows, depth = hidden.shape
    _, count, inner_width = both.shape
    each = depth // m
    first = depth // FIRST
    return pl.pallas_call(
        functools.partial(branch_back_kernel, n, m),
        name="branch_backward",
        out_shape=(
            jax.ShapeDtypeStruct((rows, depth), F32),
            jax.ShapeDtypeStruct((n * rows, width), BF),
            jax.ShapeDtypeStruct((8, depth), F32),
            jax.ShapeDtypeStruct((n, rows, depth), BF),
            jax.ShapeDtypeStruct((2 * m, each, inner_width), BF),
            jax.ShapeDtypeStruct((inner_width, each), F32),
            jax.ShapeDtypeStruct((rows, first), F32),
        ),
        in_specs=[WHOLE] * 4 + [ANY] * 6,
        out_specs=(WHOLE, WHOLE, WHOLE, ANY, ANY, WHOLE, WHOLE),
        scratch_shapes=[pltpu.VMEM((n, rows, depth), BF), pltpu.VMEM((width, depth), BF)]
        + gather_sems(n, CHUNKS)
        + [
            pltpu.SemaphoreType.DMA,
            pltpu.SemaphoreType.DMA((n,)),
            pltpu.VMEM(both.shape, BF),
            pltpu.VMEM(inner.shape, BF),
            pltpu.VMEM((2, count, each), BF),
            pltpu.VMEM((2, count, each), BF),
            pltpu.VMEM((2, each, inner_width), BF),
            pltpu.SemaphoreType.DMA((3,)),
            pltpu.SemaphoreType.DMA((2, 2)),
            pltpu.SemaphoreType.DMA((2,)),
            pltpu.VMEM((first, inner_width), BF),
        ]
        + scatter_scratch(n, rows, first, CHUNKS)
        + chip_scatter_scratch(m, (1, each, inner_width)),
        compiler_params=params(5),
        cost_estimate=cost(75),
    )(d_two, hidden, cotangent, gain, out_weights, h, both, back, inner, feed_weights)


def attend_back_kernel(
    n,
    lse_ref,
    start_ref,
    qkv_hbm,
    d_att_hbm,
    cos_hbm,
    sin_hbm,
    hidden_hbm,
    inner_hbm,
    w_hbm,
    first_ref,
    d_hbm,
    out_ref,
    part,
    inbox,
    send,
    recv,
    own,
    inner,
    down,
    key_sum,
    value_sum,
    load_sem,
    qkv_ref,
    d_att_ref,
    cos_ref,
    sin_ref,
    d_ref,
    store_sem,
):
    me = lax.axis_index("tensor")
    count, width = d_att_ref.shape
    rows_each, depth = out_ref.shape
    first = first_ref.shape[1]
    blocks = count // TILE
    loads = [
        pltpu.make_async_copy(src, dst, load_sem.at[at])
        for at, (src, dst) in enumerate(
            (
                (hidden_hbm.at[:, pl.ds(first, depth - first)], own),
                (inner_hbm, inner),
                (w_hbm.at[2, pl.ds(first, depth - first)], down),
                (qkv_hbm, qkv_ref),
                (d_att_hbm, d_att_ref),
                (cos_hbm, cos_ref),
                (sin_hbm, sin_ref),
            )
        )
    ]
    for copy in loads:
        copy.start()

    chain_barrier(me, n)
    scatter = Scatter(me, n, part, own, inbox, send, recv, FINE)
    for copy in loads[:3]:
        copy.wait()
    step_cols = 512
    for i in range(n):
        dest = nth_dest(me, n, i)

        def tile(c, carry, i=i, dest=dest):
            rows = pl.ds(pl.multiple_of(dest * rows_each, rows_each), rows_each)
            cols = pl.ds(pl.multiple_of(c * step_cols, step_cols), step_cols)
            value = nt(inner[rows], down[cols])
            if i < n - 1:
                part[dest, :, cols] = value.astype(BF)
            else:
                own[:, cols] = own[:, cols] + value
            return carry

        lax.fori_loop(0, (depth - first) // step_cols, tile, 0)
        if i < n - 1:
            scatter.offer(dest)
    for copy in loads[3:]:
        copy.wait()

    lane = lax.broadcasted_iota(jnp.int32, (TILE, LANES), 1)
    key_row = lax.broadcasted_iota(jnp.int32, (TILE, TILE), 0)
    query_lane = lax.broadcasted_iota(jnp.int32, (TILE, TILE), 1)
    diagonal = key_row <= query_lane
    scale = HEAD_DIM ** (-0.5)

    def unrotate(value, rows):
        return value * cos_ref[rows] - half_swap(value) * sin_ref[rows]

    def pair(p, carry):
        cols = pl.ds(pl.multiple_of(p * LANES, LANES), LANES)
        key_sum[...] = jnp.zeros_like(key_sum)
        value_sum[...] = jnp.zeros_like(value_sum)
        for i in range(blocks):
            rows = pl.ds(i * TILE, TILE)
            query = qkv_ref[0, rows, cols] * jnp.asarray(scale, BF)
            back = d_att_ref[rows, cols]
            begin = start_ref[0:1, rows]
            query_grad = jnp.zeros((TILE, LANES), F32)
            for e in range(2):
                ours = lane < HEAD_DIM if e == 0 else lane >= HEAD_DIM
                q = jnp.where(ours, query, jnp.zeros_like(query))
                d = jnp.where(ours, back, jnp.zeros_like(back))
                lse = lse_ref[pl.ds(2 * p + e, 1), rows]
                probs, d_probs = [], []
                centre = jnp.zeros((1, TILE), F32)
                for j in range(i + 1):
                    keys = pl.ds(j * TILE, TILE)
                    s = nt(qkv_ref[1, keys, cols], q)
                    allowed = key_row >= begin - j * TILE
                    if j == i:
                        allowed = allowed & diagonal
                    prob = jnp.where(allowed, jnp.exp(s - lse), 0.0)
                    d_prob = nt(qkv_ref[2, keys, cols], d)
                    centre = centre + jnp.sum(prob * d_prob, axis=0, keepdims=True)
                    value_sum[keys] = value_sum[keys] + nn(prob.astype(BF), d)
                    probs.append(prob)
                    d_probs.append(d_prob)
                for j in range(i + 1):
                    keys = pl.ds(j * TILE, TILE)
                    d_score = (probs[j] * (d_probs[j] - centre)).astype(BF)
                    key_sum[keys] = key_sum[keys] + nn(d_score, q)
                    k = qkv_ref[1, keys, cols]
                    query_grad = query_grad + tn(d_score, jnp.where(ours, k, jnp.zeros_like(k)))
            d_ref[0, rows, cols] = unrotate(query_grad * scale, rows).astype(BF)
            if i == blocks // 2 - 1:
                scatter.relays(5 * p // 2, 5 * p // 2 + 1)
            if i == blocks // 2:
                scatter.relays(5 * p // 2 + 1, 5 * (p + 1) // 2 - 1)
        for i in range(blocks):
            rows = pl.ds(i * TILE, TILE)
            d_ref[1, rows, cols] = unrotate(key_sum[rows], rows).astype(BF)
            d_ref[2, rows, cols] = value_sum[rows].astype(BF)
        scatter.relays(5 * (p + 1) // 2 - 1, 5 * (p + 1) // 2)
        return carry

    pairs = width // LANES
    lax.fori_loop(0, pairs, pair, 0)
    done = 5 * pairs // 2

    store = pltpu.make_async_copy(d_ref, d_hbm, store_sem)
    store.start()
    scatter.relays(done, scatter.events)
    out_ref[:, 0:first] = first_ref[...].astype(BF)
    out_ref[:, first:depth] = own[...].astype(BF)
    scatter.finish()
    store.wait()


def attend_back(n, qkv, d_att, lse, starts, cosine, sine, hidden, inner, weights, feed_first):
    _, count, width = qkv.shape
    rows, depth = hidden.shape
    inner_width = inner.shape[1]
    rest = depth - feed_first.shape[1]
    return pl.pallas_call(
        functools.partial(attend_back_kernel, n),
        name="attention_backward",
        out_shape=(
            jax.ShapeDtypeStruct((3, count, width), BF),
            jax.ShapeDtypeStruct((rows, depth), BF),
        ),
        in_specs=[WHOLE] * 2 + [ANY] * 7 + [WHOLE],
        out_specs=(ANY, WHOLE),
        scratch_shapes=scatter_scratch(n, rows, rest, FINE)
        + [
            pltpu.VMEM((rows, rest), F32),
            pltpu.VMEM((count, inner_width), BF),
            pltpu.VMEM((rest, inner_width), BF),
            pltpu.VMEM((count, LANES), F32),
            pltpu.VMEM((count, LANES), F32),
            pltpu.SemaphoreType.DMA((7,)),
            pltpu.VMEM(qkv.shape, BF),
            pltpu.VMEM(d_att.shape, BF),
            pltpu.VMEM(cosine.shape, F32),
            pltpu.VMEM(sine.shape, F32),
            pltpu.VMEM(qkv.shape, BF),
            pltpu.SemaphoreType.DMA,
        ],
        compiler_params=params(6),
        cost_estimate=cost(80),
    )(
        lse,
        starts,
        qkv,
        d_att,
        cosine,
        sine,
        hidden,
        inner,
        weights,
        feed_first,
    )


def input_back_kernel(
    n,
    m,
    d_ref,
    w_ref,
    x_ref,
    gain_ref,
    d_hidden_ref,
    gain_two_ref,
    scale_ref,
    all_x_hbm,
    h_hbm,
    branch_hbm,
    att_hbm,
    grad_ref,
    in_ref,
    out_ref,
    gain_ref_out,
    part,
    inbox,
    send,
    recv,
    own,
    gain_part,
    t_box,
    line_sum,
    d_box,
    t_send,
    t_recv,
    d_send,
    d_recv,
    att,
    h_cols,
    branch_cols,
    all_x,
    att_sem,
    x_sem,
    col_sem,
    *chip_scratch,
):
    me = lax.axis_index("tensor")
    line = lax.axis_index("dp")
    rows_each, depth = x_ref.shape
    kinds = in_ref.shape[0] + 1
    mixed_sum = ChipScatter(line, m, *chip_scratch)
    each = in_ref.shape[1]
    fetch_att = pltpu.make_async_copy(att_hbm, att, att_sem)
    fetch_x = pltpu.make_async_copy(all_x_hbm, all_x, x_sem)
    fetch_x.start()
    fetch_att.start()

    def fetch_cols(at):
        cols = pl.ds(pl.multiple_of(mixed_sum.target(at) * each, each), each)
        return (
            pltpu.make_async_copy(h_hbm.at[:, cols], h_cols.at[at % 2], col_sem.at[0, at % 2]),
            pltpu.make_async_copy(branch_hbm.at[:, cols], branch_cols.at[at % 2], col_sem.at[1, at % 2]),
        )

    for copy in fetch_cols(0):
        copy.start()
    everyone_barrier(me, n, line, m)
    scatter = Scatter(me, n, part, own, inbox, send, recv, FINE)
    own[...] = jnp.zeros_like(own)
    gain_part[...] = gain_two_ref[...]
    fetch_x.wait()
    step_cols = 512

    def term(i):
        dest = nth_dest(me, n, i)

        def tile(c, carry):
            rows = pl.ds(pl.multiple_of(dest * rows_each, rows_each), rows_each)
            cols = pl.ds(pl.multiple_of(c * step_cols, step_cols), step_cols)
            value = nt(d_ref[0, rows], w_ref[0, cols])
            for kind in range(1, 3):
                value = value + nt(d_ref[kind, rows], w_ref[kind, cols])
            if i < n - 1:
                part[dest, :, cols] = value.astype(BF)
            else:
                own[:, cols] = own[:, cols] + value
            normed = all_x[rows, cols].astype(F32) * scale_ref[rows, 0:1]
            gain_part[0:1, cols] = gain_part[0:1, cols] + jnp.sum(value * normed, axis=0, keepdims=True)
            return carry

        lax.fori_loop(0, depth // step_cols, tile, 0)
        if i < n - 1:
            scatter.offer(dest)

    term(0)
    term(1)
    def across(hop):
        return pltpu.make_async_remote_copy(
            src_ref=gain_part,
            dst_ref=t_box.at[hop],
            send_sem=t_send.at[hop],
            recv_sem=t_recv.at[hop],
            device_id={"tensor": lax.rem(me + hop, n)},
            device_id_type=MESH,
        )

    def along(hop):
        to = lax.rem(line + hop, m)
        return pltpu.make_async_remote_copy(
            src_ref=line_sum.at[to],
            dst_ref=d_box.at[hop],
            send_sem=d_send.at[hop],
            recv_sem=d_recv.at[hop],
            device_id={"dp": to},
            device_id_type=MESH,
        )

    fetch_att.wait()
    served = 0
    for at in range(m):
        if at + 1 < m:
            for copy in fetch_cols(at + 1):
                copy.start()
        for copy in fetch_cols(at):
            copy.wait()
        h_turned = jnp.transpose(h_cols[at % 2])
        branch_turned = jnp.transpose(branch_cols[at % 2])
        to = mixed_sum.slot(at)
        for kind in range(kinds):
            value = nn(h_turned, d_ref[kind]) if kind < kinds - 1 else nn(branch_turned, att[...])
            to[kind] = value.astype(BF)
        mixed_sum.filled(at)
        if 4 * (at + 1) // m - 1 > served:
            scatter.relay(served)
            served += 1
    mixed_sum.combine(0)
    for i in range(2, n):
        term(i)
    for hop in range(1, n):
        across(hop).start()
    scatter.relays(served, served + 1)
    mixed_sum.forward()
    scatter.relays(served + 1, served + 3)
    for hop in range(1, n):
        across(hop).wait_recv()
    gain_total = gain_part[...]
    for hop in range(1, n):
        gain_total = gain_total + t_box[hop]
    gain_width = gain_ref_out.shape[1]
    for at in range(m):
        line_sum[at] = gain_total[:, at * gain_width : (at + 1) * gain_width]
    for hop in range(1, m):
        along(hop).start()
    scatter.relays(served + 3, scatter.events)
    step_rows = min(LANES, rows_each)

    def norm(r, carry):
        rows = pl.ds(pl.multiple_of(r * step_rows, step_rows), step_rows)
        x = x_ref[rows].astype(F32)
        scale = row_scale(x)
        normed = x * scale
        d_one = own[rows]
        scaled = d_one * gain_ref[0:1]
        back = scale * (scaled - normed * jnp.mean(scaled * normed, axis=-1, keepdims=True))
        grad_ref[rows] = d_hidden_ref[rows] + back
        return carry

    lax.fori_loop(0, rows_each // step_rows, norm, 0)
    for hop in range(1, m):
        along(hop).wait_recv()
    result = line_sum[line]
    for hop in range(1, m):
        result = result + d_box[hop]
    gain_ref_out[...] = result
    mixed_sum.arrive()
    for kind in range(kinds):
        total = mixed_sum.result(kind)
        if kind < kinds - 1:
            in_ref[kind] = total
        else:
            out_ref[...] = jnp.transpose(total)

    scatter.finish()
    for hop in range(1, n):
        across(hop).wait_send()
    for hop in range(1, m):
        along(hop).wait_send()
    mixed_sum.finish()


def input_back(
    n, m, d_projected, weights, x, gain, d_hidden, gain_two, scale, all_x, h, d_branch, attended
):
    rows, depth = x.shape
    kinds = d_projected.shape[0] + 1
    each = depth // m
    count, width = attended.shape
    shard = (kinds, each, width)
    return pl.pallas_call(
        functools.partial(input_back_kernel, n, m),
        name="input_backward",
        out_shape=(
            jax.ShapeDtypeStruct((rows, depth), F32),
            jax.ShapeDtypeStruct((kinds - 1, each, width), F32),
            jax.ShapeDtypeStruct((width, each), F32),
            jax.ShapeDtypeStruct((8, each), F32),
        ),
        in_specs=[WHOLE] * 7 + [ANY] * 4,
        out_specs=(WHOLE,) * 4,
        scratch_shapes=scatter_scratch(n, rows, depth, FINE)
        + [pltpu.VMEM((rows, depth), F32)]
        + [
            pltpu.VMEM((8, depth), F32),
            pltpu.VMEM((n, 8, depth), F32),
            pltpu.VMEM((m, 8, each), F32),
            pltpu.VMEM((m, 8, each), F32),
            pltpu.SemaphoreType.DMA((n,)),
            pltpu.SemaphoreType.DMA((n,)),
            pltpu.SemaphoreType.DMA((m,)),
            pltpu.SemaphoreType.DMA((m,)),
            pltpu.VMEM((count, width), BF),
            pltpu.VMEM((2, count, each), BF),
            pltpu.VMEM((2, count, each), BF),
            pltpu.VMEM((count, depth), BF),
            pltpu.SemaphoreType.DMA,
            pltpu.SemaphoreType.DMA,
            pltpu.SemaphoreType.DMA((2, 2)),
        ]
        + chip_scatter_scratch(m, shard),
        compiler_params=params(7),
        cost_estimate=cost(75),
    )(
        d_projected,
        weights,
        x,
        gain,
        d_hidden,
        gain_two,
        scale,
        all_x,
        h,
        d_branch,
        attended,
    )


def adam_kernel(rate, decay, w_ref, first_ref, second_ref, grad_ref, first_out, second_out, w_out):
    for kind in range(2):
        new = adam_step(
            w_ref[:, kind, :],
            first_ref[:, kind, :],
            second_ref[:, kind, :],
            grad_ref[kind].astype(F32),
            rate,
            decay,
        )
        first_out[:, kind, :] = new[0]
        second_out[:, kind, :] = new[1]
        w_out[:, kind, :] = new[2]


def adam_pair(weight, first, second, grad, rate, decay):
    rows, kinds, width = weight.shape
    step = 64
    spec = pl.BlockSpec((step, kinds, width), lambda i: (i, 0, 0))
    shape = jax.ShapeDtypeStruct(weight.shape, F32)
    return pl.pallas_call(
        functools.partial(adam_kernel, rate, decay),
        name="adam_gate_up",
        grid=(rows // step,),
        out_shape=(shape,) * 3,
        in_specs=[spec] * 3 + [pl.BlockSpec((kinds, step, width), lambda i: (0, i, 0))],
        out_specs=(spec,) * 3,
        compiler_params=params(),
        cost_estimate=cost(10),
    )(weight, first, second, grad)


def rows_first(array):
    return with_layout_constraint(array, Layout(major_to_minor=tuple(range(array.ndim))))


def adam_step(weight, first_moment, second_moment, grad, rate, decay):
    new_first = BETA_ONE * first_moment + (1.0 - BETA_ONE) * grad
    new_second = BETA_TWO * second_moment + (1.0 - BETA_TWO) * grad * grad
    mean_part = new_first / (1.0 - BETA_ONE**STEP)
    size_part = jnp.sqrt(new_second / (1.0 - BETA_TWO**STEP)) + ADAM_EPSILON
    new_weight = weight - rate * (mean_part / size_part + decay * weight)
    return (new_first, new_second, new_weight)


def local(
    n,
    m,
    tokens,
    cotangent,
    doc_start,
    in_weight,
    in_first,
    in_second,
    out_weight,
    out_first,
    out_second,
    gate_up,
    gate_up_first,
    gate_up_second,
    down_weight,
    down_first,
    down_second,
    norm_gains,
    gains_first,
    gains_second,
):
    count = doc_start.shape[0]
    depth = tokens.shape[1]

    in_low = jnp.transpose(in_weight, (1, 0, 2)).astype(BF)
    gain_low = jnp.pad(lax.reduce_precision(norm_gains, 8, 7), ((0, 6), (0, 0)))
    powers = jnp.arange(HEAD_DIM // 2, dtype=F32) * (2.0 / HEAD_DIM)
    freqs = jnp.broadcast_to(jnp.tile(ROPE_BASE ** (-powers), 4)[None, :], (8, LANES))
    start_rows = jnp.broadcast_to(doc_start[:, None], (count, LANES))
    start_lanes = jnp.broadcast_to(doc_start[None, :], (8, count))

    in_w = lax.all_gather(in_low, "dp", axis=1, tiled=True)
    out_line, gain_line = gather_first(n, m, out_weight.astype(BF), gain_low)
    gains = jnp.transpose(gain_line, (1, 0, 2)).reshape(8, depth)
    out_line = out_line.reshape(depth, out_line.shape[2])
    out_w = lax.all_gather(out_line, "dp", axis=1, tiled=True)

    own_tokens, _ = lax.optimization_barrier((tokens, gains))
    x, feed_low, cosine, sine = gather_rows(n, own_tokens, gate_up, down_weight, start_rows, freqs)
    x = x.reshape(count, depth)
    feed_w = lax.all_gather(feed_low, "dp", axis=1, tiled=True)

    h_one, qkv, attended, lse, scale_one, back = attend(
        n, x, gains, in_w, cosine, sine, start_rows, cotangent
    )
    back = back.reshape(count, depth)
    h_two, hidden = project_branch(n, attended, out_w, x, gains)
    inner, d_both, d_two = feed(n, h_two, back, feed_w)
    d_hidden, d_att, gain_two, d_branch, up_grad, down_summed, feed_first = branch_back(
        n,
        m,
        d_two,
        hidden,
        cotangent,
        gains,
        out_w,
        h_two,
        d_both,
        back,
        inner,
        feed_w,
        attended.shape[1],
    )
    up_summed = rows_first(lax.psum_scatter(up_grad, "dp", scatter_dimension=0, tiled=True))
    d_projected, output = attend_back(
        n, qkv, d_att, lse, start_lanes, cosine, sine, hidden, inner, feed_w, feed_first
    )
    input_grad, in_summed, out_summed, gain_summed = input_back(
        n,
        m,
        d_projected,
        in_w,
        tokens,
        gains,
        d_hidden,
        gain_two,
        scale_one,
        x,
        h_one,
        d_branch.reshape(count, depth),
        attended,
    )
    up_new = tuple(
        adam_pair(
            gate_up, gate_up_first, gate_up_second, up_summed, 2.0 * D ** (-0.5), WEIGHT_DECAY
        )
    )
    down_new = adam_step(
        down_weight, down_first, down_second, down_summed, 2.0 * FF ** (-0.5), WEIGHT_DECAY
    )
    in_new = adam_step(
        in_weight, in_first, in_second, jnp.transpose(in_summed, (1, 0, 2)), 2.0 * D ** (-0.5), WEIGHT_DECAY
    )
    out_new = adam_step(
        out_weight, out_first, out_second, out_summed, 2.0 * (D // 8) ** (-0.5), WEIGHT_DECAY
    )
    gain_new = adam_step(norm_gains, gains_first, gains_second, gain_summed[0:2], GAIN_RATE, 0.0)
    return (output, input_grad) + in_new + out_new + up_new + down_new + gain_new


def solution(mesh):
    rows = P(("dp", "tensor"), None)
    wide = P("dp", None, "tensor")
    tall = P("tensor", "dp")
    gains = P(None, "dp")
    in_specs = (rows, rows, P("dp")) + (wide,) * 3 + (tall,) * 3 + (wide,) * 3 + (tall,) * 3 + (gains,) * 3
    out_specs = (rows, rows) + (wide,) * 3 + (tall,) * 3 + (wide,) * 3 + (tall,) * 3 + (gains,) * 3
    return jax.shard_map(
        functools.partial(local, mesh.shape["tensor"], mesh.shape["dp"]),
        mesh=mesh,
        in_specs=in_specs,
        out_specs=out_specs,
        check_vma=False,
    )
```

```python
import functools

import jax
import jax.numpy as jnp
from jax import lax
from jax.experimental.layout import Layout, with_layout_constraint
from jax.experimental import pallas as pl
from jax.experimental.pallas import tpu as pltpu
from jax.sharding import PartitionSpec as P

D = 2048
HEAD_DIM = 64
FF = 8192
STEP = 5


EPSILON = 1e-05
ROPE_BASE = 130000.0
BETA_ONE = 0.9
BETA_TWO = 0.95
ADAM_EPSILON = 1e-08
WEIGHT_DECAY = 0.1
GAIN_RATE = 0.5
MASK_VALUE = -1e30

MESH = pl.DeviceIdType.MESH
BF = jnp.bfloat16
F32 = jnp.float32
TILE = 256
LANES = 128
CHUNKS = 2
FINE = 4
FIRST = 4
VMEM_LIMIT = 60 * 1024 * 1024

WHOLE = pl.BlockSpec(memory_space=pltpu.VMEM)
ANY = pl.BlockSpec(memory_space=pl.ANY)


def nn(a, b):
    return lax.dot_general(a, b, (((1,), (0,)), ((), ())), preferred_element_type=F32)


def nt(a, b):
    return lax.dot_general(a, b, (((1,), (1,)), ((), ())), preferred_element_type=F32)


def tn(a, b):
    return lax.dot_general(a, b, (((0,), (0,)), ((), ())), preferred_element_type=F32)


def params(collective_id=None):
    if collective_id is None:
        return pltpu.CompilerParams(vmem_limit_bytes=VMEM_LIMIT)
    return pltpu.CompilerParams(
        vmem_limit_bytes=VMEM_LIMIT, collective_id=collective_id, has_side_effects=True
    )


def cost(microseconds):
    return pl.CostEstimate(
        flops=int(microseconds * 1.0e9), bytes_accessed=int(microseconds * 2.0e6), transcendentals=0
    )


def neighbours(me, n):
    return (me > 0).astype(jnp.int32) + (me < n - 1).astype(jnp.int32)


def chain_barrier(me, n):
    barrier = pltpu.get_barrier_semaphore()
    for there, other in ((me > 0, me - 1), (me < n - 1, me + 1)):

        @pl.when(there)
        def _(other=other):
            pl.semaphore_signal(barrier, inc=1, device_id={"tensor": other}, device_id_type=MESH)

    pl.semaphore_wait(barrier, neighbours(me, n))


def chips_barrier(me, n, line, m):
    chips = m // 2
    chip, core = line // 2, lax.rem(line, 2)
    barrier = pltpu.get_barrier_semaphore()
    for there, other in ((me > 0, me - 1), (me < n - 1, me + 1)):

        @pl.when(there)
        def _(other=other):
            pl.semaphore_signal(barrier, inc=1, device_id={"tensor": other}, device_id_type=MESH)

    pl.semaphore_signal(barrier, inc=1, device_id={"dp": 2 * chip + 1 - core}, device_id_type=MESH)
    for hop in range(1, chips):
        to = 2 * lax.rem(chip + hop, chips) + core
        pl.semaphore_signal(barrier, inc=1, device_id={"dp": to}, device_id_type=MESH)
    pl.semaphore_wait(barrier, neighbours(me, n) + chips)


def everyone_barrier(me, n, line, m):
    barrier = pltpu.get_barrier_semaphore()
    for hop in range(1, n):
        to = lax.rem(me + hop, n)
        pl.semaphore_signal(barrier, inc=1, device_id={"tensor": to}, device_id_type=MESH)
    for hop in range(1, m):
        to = lax.rem(line + hop, m)
        pl.semaphore_signal(barrier, inc=1, device_id={"dp": to}, device_id_type=MESH)
    pl.semaphore_wait(barrier, n + m - 2)


class Gather:
    def __init__(self, me, n, own, place, send, recv, chunks):
        self.me, self.n, self.own, self.place = me, n, own, place
        self.send, self.recv, self.chunks = send, recv, chunks

    def link(self, way, step, c):
        shard = self.me - step if way == 0 else self.me + step
        to = self.me + 1 if way == 0 else self.me - 1
        dst = self.place(shard, c)
        return pltpu.make_async_remote_copy(
            src_ref=self.own(c) if step == 0 else dst,
            dst_ref=dst,
            send_sem=self.send.at[way, step, c],
            recv_sem=self.recv.at[way, step, c],
            device_id={"tensor": to},
            device_id_type=MESH,
        )

    def holds(self, way, step):
        return self.me - step >= 0 if way == 0 else self.me + step <= self.n - 1

    def passes(self, way):
        return self.me < self.n - 1 if way == 0 else self.me > 0

    def start(self):
        for c in range(self.chunks):
            for way in range(2):

                @pl.when(self.passes(way))
                def _(way=way, c=c):
                    self.link(way, 0, c).start()

    def advance(self, step, only=None):
        for c in range(self.chunks) if only is None else (only,):
            for way in range(2):

                @pl.when(self.holds(way, step))
                def _(way=way, c=c):
                    shard = self.me - step if way == 0 else self.me + step
                    here = self.place(shard, c)
                    pltpu.make_async_remote_copy(
                        src_ref=here,
                        dst_ref=here,
                        send_sem=self.send.at[way, step - 1, c],
                        recv_sem=self.recv.at[way, step - 1, c],
                        device_id={"tensor": self.me},
                        device_id_type=MESH,
                    ).wait_recv()
                    if step < self.n - 1:

                        @pl.when(self.passes(way))
                        def _():
                            self.link(way, step, c).start()

    def finish(self):
        for step in range(self.n - 1):
            for c in range(self.chunks):
                for way in range(2):

                    @pl.when(self.holds(way, step) & self.passes(way))
                    def _(way=way, c=c, step=step):
                        self.link(way, step, c).wait_send()


def gather_sems(n, chunks):
    return [pltpu.SemaphoreType.DMA((2, n - 1, chunks)), pltpu.SemaphoreType.DMA((2, n - 1, chunks))]


def nth_dest(me, n, i):
    if i == n - 1:
        return me
    both = jnp.minimum(me, n - 1 - me)
    near = jnp.where((me < n // 2) == (i % 2 == 0), n - 1 - i // 2, i // 2)
    late = i - both
    return jnp.where(i < 2 * both, near, jnp.where(n - 1 - me > me, n - 1 - late, late))


class Scatter:
    def __init__(self, me, n, part, own, inbox, send, recv, chunks):
        self.me, self.n, self.part, self.own, self.inbox = me, n, part, own, inbox
        self.send, self.recv, self.chunks = send, recv, chunks
        self.size = part.shape[1] // chunks
        self.events = (n - 1) * chunks + n - 2

    def rows(self, c):
        return pl.ds(pl.multiple_of(c * self.size, self.size), self.size)

    def box(self, way, step, c):
        return self.inbox.at[step if way == 0 else self.n - step, self.rows(c)]

    def hop(self, way, dest, c):
        step = self.n - 1 - dest if way == 0 else dest
        return pltpu.make_async_remote_copy(
            src_ref=self.part.at[dest, self.rows(c)],
            dst_ref=self.box(way, step, c),
            send_sem=self.send.at[way, step, c],
            recv_sem=self.recv.at[way, step, c],
            device_id={"tensor": self.me + 1 if way == 0 else self.me - 1},
            device_id_type=MESH,
        )

    def offer(self, dest):
        for way in range(2):
            first = (self.me == 0) & (dest > self.me) if way == 0 else (self.me == self.n - 1) & (dest < self.me)

            @pl.when(first)
            def _(way=way):
                for c in range(self.chunks):
                    self.hop(way, dest, c).start()

    def relay(self, time):
        for way in range(2):
            number = time - (self.me - 1) if way == 0 else time - (self.n - 2 - self.me)
            inside = (number >= 0) & (number < (self.n - 1) * self.chunks)
            number = jnp.where(inside, number, 0)
            step = number // self.chunks
            c = number - step * self.chunks
            dest = self.n - 1 - step if way == 0 else step
            if way == 0:
                live = inside & (self.me > 0) & (dest >= self.me)
            else:
                live = inside & (self.me < self.n - 1) & (dest <= self.me)

            @pl.when(live)
            def _(way=way, step=step, c=c, dest=dest):
                here = self.box(way, step, c)
                pltpu.make_async_remote_copy(
                    src_ref=here,
                    dst_ref=here,
                    send_sem=self.send.at[way, step, c],
                    recv_sem=self.recv.at[way, step, c],
                    device_id={"tensor": self.me},
                    device_id_type=MESH,
                ).wait_recv()
                rows = self.rows(c)

                @pl.when(dest == self.me)
                def _():
                    self.own[rows] = self.own[rows] + here[...].astype(F32)

                @pl.when(dest != self.me)
                def _():
                    self.part[dest, rows] = self.part[dest, rows] + here[...]
                    self.hop(way, dest, c).start()

    def relays(self, first, last):
        def body(time, carry):
            self.relay(time)
            return carry

        lax.fori_loop(first, last, body, 0)

    def finish(self):
        for step in range(self.n - 1):
            for c in range(self.chunks):
                for way in range(2):
                    dest = self.n - 1 - step if way == 0 else step

                    @pl.when(self.me < dest if way == 0 else self.me > dest)
                    def _(way=way, dest=dest, c=c):
                        self.hop(way, dest, c).wait_send()


def scatter_scratch(n, rows, width, chunks):
    return [
        pltpu.VMEM((n, rows, width), BF),
        pltpu.VMEM((n + 1, rows, width), BF),
        pltpu.SemaphoreType.DMA((2, n - 1, chunks)),
        pltpu.SemaphoreType.DMA((2, n - 1, chunks)),
    ]


class ChipScatter:
    def __init__(self, line, m, early, mine, theirs, half, box, pair_send, pair_recv, chip_send, chip_recv):
        self.early = early
        self.chips = m // 2
        self.square = self.chips == 4
        self.chip, self.core = line // 2, lax.rem(line, 2)
        self.mine, self.theirs, self.half, self.box = mine, theirs, half, box
        self.pair_send, self.pair_recv = pair_send, pair_recv
        self.chip_send, self.chip_recv = chip_send, chip_recv
        self.kinds, self.size = mine.shape[1], mine.shape[2]
        order = [3, 1, 2, 0] if self.square else list(range(1, self.chips)) + [0]
        self.steps = [(hop, other) for hop in order for other in (True, False)]

    def device(self, hop, core):
        if self.square:
            x, y = lax.rem(self.chip, 2), self.chip // 2
            return 2 * (2 * lax.rem(y + hop // 2, 2) + lax.rem(x + hop % 2, 2)) + core
        return 2 * lax.rem(self.chip + hop, self.chips) + core

    def target(self, at):
        hop, other = self.steps[at]
        return self.device(hop, 1 - self.core if other else self.core)

    def slot(self, at):
        hop, other = self.steps[at]
        return self.theirs.at[hop] if other else self.mine.at[hop]

    def to_pair(self, hop):
        return pltpu.make_async_remote_copy(
            src_ref=self.theirs.at[hop],
            dst_ref=self.half.at[hop],
            send_sem=self.pair_send.at[hop],
            recv_sem=self.pair_recv.at[hop],
            device_id={"dp": 2 * self.chip + 1 - self.core},
            device_id_type=MESH,
        )

    def to_chip(self, hop):
        return pltpu.make_async_remote_copy(
            src_ref=self.mine.at[hop],
            dst_ref=self.box.at[hop],
            send_sem=self.chip_send.at[hop],
            recv_sem=self.chip_recv.at[hop],
            device_id={"dp": self.device(hop, self.core)},
            device_id_type=MESH,
        )

    def over(self, hop):
        rows = pl.ds((hop - 1) * self.size // 2, self.size // 2)
        sem = 3 if hop == 1 else 0
        return pltpu.make_async_remote_copy(
            src_ref=self.mine.at[3, :, rows],
            dst_ref=self.box.at[3, :, rows],
            send_sem=self.chip_send.at[sem],
            recv_sem=self.chip_recv.at[sem],
            device_id={"dp": self.device(hop, self.core)},
            device_id_type=MESH,
        )

    def filled(self, at):
        hop, other = self.steps[at]
        if other:
            self.to_pair(hop).start()
        if at >= 2 and other == self.early:
            self.combine(self.steps[at - 1 if self.early else at - 2][0])

    def combine(self, hop):
        self.to_pair(hop).wait_recv()
        for kind in range(self.kinds):
            self.mine[hop, kind] = self.mine[hop, kind] + self.half[hop, kind]
        if not self.square:
            if hop > 0:
                self.to_chip(hop).start()
        elif hop == 3:
            self.over(1).start()
            self.over(2).start()

    def forward(self):
        if not self.square:
            return
        for via, hop in ((1, 2), (2, 1)):
            self.over(via).wait_recv()
            rows = pl.ds((via - 1) * self.size // 2, self.size // 2)
            for kind in range(self.kinds):
                self.mine[hop, kind, rows] = self.mine[hop, kind, rows] + self.box[3, kind, rows]
            self.to_chip(hop).start()

    def final(self):
        return (1, 2) if self.square else tuple(range(1, self.chips))

    def arrive(self):
        for hop in self.final():
            self.to_chip(hop).wait_recv()

    def result(self, kind):
        total = self.mine[0, kind].astype(F32)
        for hop in self.final():
            total = total + self.box[hop, kind].astype(F32)
        return total

    def finish(self):
        for hop in range(self.chips):
            self.to_pair(hop).wait_send()
        for hop in self.final():
            self.to_chip(hop).wait_send()
        if self.square:
            self.over(1).wait_send()
            self.over(2).wait_send()


def chip_scatter_scratch(m, shard):
    return [pltpu.VMEM((m // 2,) + shard, BF)] * 4 + [pltpu.SemaphoreType.DMA((m // 2,))] * 4


def half_swap(values):
    lane = lax.broadcasted_iota(jnp.int32, values.shape, 1)
    lower = lax.rem(lane, HEAD_DIM) < HEAD_DIM // 2
    return jnp.where(
        lower, pltpu.roll(values, LANES - HEAD_DIM // 2, 1), pltpu.roll(values, HEAD_DIM // 2, 1)
    )


def row_scale(values):
    return lax.rsqrt(jnp.mean(values * values, axis=-1, keepdims=True) + EPSILON)


def first_kernel(n, m, out_ref, gain_ref, all_out, all_gain, send, recv, gain_send, gain_recv, local_sem):
    me = lax.axis_index("tensor")
    line = lax.axis_index("dp")
    barrier = pltpu.get_barrier_semaphore()
    for hop in range(1, m):
        pl.semaphore_signal(
            barrier, inc=1, device_id={"dp": lax.rem(line + hop, m)}, device_id_type=MESH
        )
    for there, other in ((me > 0, me - 1), (me < n - 1, me + 1)):

        @pl.when(there)
        def _(other=other):
            pl.semaphore_signal(barrier, inc=1, device_id={"tensor": other}, device_id_type=MESH)

    pl.semaphore_wait(barrier, m - 1 + neighbours(me, n))

    size = out_ref.shape[0] // CHUNKS
    gather = Gather(
        me,
        n,
        lambda c: out_ref.at[pl.ds(c * size, size)],
        lambda shard, c: all_out.at[shard, pl.ds(c * size, size)],
        send,
        recv,
        CHUNKS,
    )
    gather.start()

    def gain_copy(hop):
        return pltpu.make_async_remote_copy(
            src_ref=gain_ref,
            dst_ref=all_gain.at[line],
            send_sem=gain_send.at[hop],
            recv_sem=gain_recv.at[hop],
            device_id={"dp": lax.rem(line + hop, m)},
            device_id_type=MESH,
        )

    for hop in range(1, m):
        gain_copy(hop).start()
    mine = pltpu.make_async_copy(out_ref, all_out.at[me], local_sem.at[0])
    mine.start()
    mine_gain = pltpu.make_async_copy(gain_ref, all_gain.at[line], local_sem.at[1])
    mine_gain.start()
    for step in range(1, n):
        gather.advance(step)
    for hop in range(1, m):
        source = lax.rem(line + m - hop, m)
        pltpu.make_async_remote_copy(
            src_ref=gain_ref,
            dst_ref=all_gain.at[source],
            send_sem=gain_send.at[hop],
            recv_sem=gain_recv.at[hop],
            device_id={"dp": source},
            device_id_type=MESH,
        ).wait_recv()
    for hop in range(1, m):
        gain_copy(hop).wait_send()
    gather.finish()
    mine.wait()
    mine_gain.wait()


def gather_first(n, m, out_low, gains):
    rows, width = out_low.shape
    return pl.pallas_call(
        functools.partial(first_kernel, n, m),
        name="gather_out_shards",
        out_shape=(
            jax.ShapeDtypeStruct((n, rows, width), BF),
            jax.ShapeDtypeStruct((m,) + gains.shape, F32),
        ),
        in_specs=[ANY, ANY],
        out_specs=(ANY, ANY),
        scratch_shapes=gather_sems(n, CHUNKS)
        + [
            pltpu.SemaphoreType.DMA((m,)),
            pltpu.SemaphoreType.DMA((m,)),
            pltpu.SemaphoreType.DMA((2,)),
        ],
        compiler_params=params(0),
        cost_estimate=cost(20),
    )(out_low, gains)


def rows_kernel(
    n,
    x_ref,
    up_hbm,
    down_hbm,
    start_ref,
    freq_ref,
    all_x,
    low_ref,
    cos_ref,
    sin_ref,
    send,
    recv,
    up,
    down,
    local_sem,
    load_sem,
):
    me = lax.axis_index("tensor")
    size = x_ref.shape[0] // CHUNKS
    loads = (
        pltpu.make_async_copy(up_hbm, up, load_sem.at[0]),
        pltpu.make_async_copy(down_hbm, down, load_sem.at[1]),
    )
    for copy in loads:
        copy.start()
    chain_barrier(me, n)
    gather = Gather(
        me,
        n,
        lambda c: x_ref.at[pl.ds(c * size, size)],
        lambda shard, c: all_x.at[shard, pl.ds(c * size, size)],
        send,
        recv,
        CHUNKS,
    )
    gather.start()
    mine = pltpu.make_async_copy(x_ref, all_x.at[me], local_sem)
    mine.start()
    for copy in loads:
        copy.wait()
    hidden, each = down.shape

    def cast(r, carry):
        rows = pl.ds(pl.multiple_of(r * 32, 32), 32)
        for kind in range(2):
            low_ref[kind, rows] = up[rows, kind, :].astype(BF)
        return carry

    lax.fori_loop(0, each // 32, cast, 0)

    def turn(c, carry):
        cols = pl.ds(pl.multiple_of(c * TILE, TILE), TILE)
        low_ref[2, :, cols] = jnp.transpose(down[cols]).astype(BF)
        return carry

    lax.fori_loop(0, hidden // TILE, turn, 0)
    gather.advance(1)

    def table(r, carry):
        rows = pl.ds(pl.multiple_of(r * 64, 64), 64)
        place = lax.broadcasted_iota(jnp.int32, (64, LANES), 0) + r * 64 - start_ref[rows]
        lane = lax.broadcasted_iota(jnp.int32, (64, LANES), 1)
        angle = place.astype(F32) * freq_ref[0:1]
        cos_ref[rows] = jnp.cos(angle)
        sine = jnp.sin(angle)
        sin_ref[rows] = jnp.where(lax.rem(lane, HEAD_DIM) < HEAD_DIM // 2, -sine, sine)
        return carry

    lax.fori_loop(0, cos_ref.shape[0] // 64, table, 0)
    for step in range(2, n):
        gather.advance(step)
    gather.finish()
    mine.wait()


def gather_rows(n, x, gate_up, down_weight, starts, freqs):
    each, _, hidden = gate_up.shape
    table = jax.ShapeDtypeStruct(starts.shape, F32)
    return pl.pallas_call(
        functools.partial(rows_kernel, n),
        name="gather_tokens",
        out_shape=(
            jax.ShapeDtypeStruct((n,) + x.shape, BF),
            jax.ShapeDtypeStruct((3, each, hidden), BF),
            table,
            table,
        ),
        in_specs=[ANY] * 3 + [WHOLE] * 2,
        out_specs=(ANY, WHOLE, WHOLE, WHOLE),
        scratch_shapes=gather_sems(n, CHUNKS)
        + [
            pltpu.VMEM(gate_up.shape, F32),
            pltpu.VMEM(down_weight.shape, F32),
            pltpu.SemaphoreType.DMA,
            pltpu.SemaphoreType.DMA((2,)),
        ],
        compiler_params=params(1),
        cost_estimate=cost(65),
    )(x, gate_up, down_weight, starts, freqs)


def attend_kernel(
    n,
    x_hbm,
    gain_ref,
    w_hbm,
    cos_ref,
    sin_ref,
    start_ref,
    back_ref,
    h_hbm,
    qkv_hbm,
    att_hbm,
    lse_ref,
    scale_ref,
    all_back,
    send,
    recv,
    local_sem,
    x_ref,
    w_ref,
    h_ref,
    qkv_ref,
    att_ref,
    move_sem,
):
    me = lax.axis_index("tensor")
    count = x_ref.shape[0]
    width = w_ref.shape[2]
    blocks = count // TILE
    moves = [
        pltpu.make_async_copy(src, dst, move_sem.at[at])
        for at, (src, dst) in enumerate(
            ((x_hbm, x_ref), (w_hbm, w_ref), (h_ref, h_hbm), (qkv_ref, qkv_hbm), (att_ref, att_hbm))
        )
    ]
    moves[0].start()
    moves[1].start()
    size = back_ref.shape[0] // CHUNKS
    chain_barrier(me, n)
    gather = Gather(
        me,
        n,
        lambda c: back_ref.at[pl.ds(c * size, size)],
        lambda shard, c: all_back.at[shard, pl.ds(c * size, size)],
        send,
        recv,
        CHUNKS,
    )
    gather.start()
    mine = pltpu.make_async_copy(back_ref, all_back.at[me], local_sem)
    mine.start()

    def project(r, carry):
        rows = pl.ds(pl.multiple_of(r * TILE, TILE), TILE)
        x = x_ref[rows].astype(F32)
        scale = row_scale(x)
        scale_ref[rows] = jnp.broadcast_to(scale, (TILE, LANES))
        h = (x * scale * gain_ref[0:1]).astype(BF)
        h_ref[rows] = h
        cosine, sine = cos_ref[rows], sin_ref[rows]
        for kind in range(3):
            value = nn(h, w_ref[kind])
            if kind < 2:
                value = jnp.concatenate(
                    [
                        value[:, c : c + LANES] * cosine + half_swap(value[:, c : c + LANES]) * sine
                        for c in range(0, width, LANES)
                    ],
                    axis=1,
                )
            qkv_ref[kind, rows] = value.astype(BF)
        return carry

    moves[0].wait()
    moves[1].wait()
    lax.fori_loop(0, blocks, project, 0)
    moves[2].start()
    moves[3].start()

    lane = lax.broadcasted_iota(jnp.int32, (TILE, LANES), 1)
    key_lane = lax.broadcasted_iota(jnp.int32, (TILE, TILE), 1)
    query_row = lax.broadcasted_iota(jnp.int32, (TILE, TILE), 0)
    diagonal = key_lane <= query_row

    def pair(p, carry):
        cols = pl.ds(pl.multiple_of(p * LANES, LANES), LANES)
        for i in range(blocks):
            rows = pl.ds(i * TILE, TILE)
            query = qkv_ref[0, rows, cols] * jnp.asarray(HEAD_DIM ** (-0.5), BF)
            begin = start_ref[rows, 0:1]
            result = jnp.zeros((TILE, LANES), F32)
            for e in range(2):
                ours = lane < HEAD_DIM if e == 0 else lane >= HEAD_DIM
                q = jnp.where(ours, query, jnp.zeros_like(query))
                scores = []
                for j in range(i + 1):
                    s = nt(q, qkv_ref[1, pl.ds(j * TILE, TILE), cols])
                    allowed = key_lane >= begin - j * TILE
                    if j == i:
                        allowed = allowed & diagonal
                    scores.append(jnp.where(allowed, s, MASK_VALUE))
                top = functools.reduce(jnp.maximum, scores)
                peak = jnp.max(top, axis=-1, keepdims=True)
                expo = [jnp.exp(s - peak) for s in scores]
                total = jnp.sum(functools.reduce(jnp.add, expo), axis=-1, keepdims=True)
                acc = jnp.zeros((TILE, LANES), F32)
                for j in range(i + 1):
                    v = qkv_ref[2, pl.ds(j * TILE, TILE), cols]
                    acc = acc + nn(expo[j].astype(BF), jnp.where(ours, v, jnp.zeros_like(v)))
                result = result + acc / total
                lse = jnp.broadcast_to(peak + jnp.log(total), (TILE, LANES))
                lse_ref[pl.ds(2 * p + e, 1), rows] = jnp.transpose(lse)[0:1]
            att_ref[rows, cols] = result.astype(BF)
        return carry

    pairs = width // LANES
    lax.fori_loop(0, pairs // 2, pair, 0)
    gather.advance(1)
    lax.fori_loop(pairs // 2, pairs, pair, 0)
    moves[4].start()
    for step in range(2, n):
        gather.advance(step)
    gather.finish()
    mine.wait()
    for move in moves[2:]:
        move.wait()


def attend(n, x, gain, weights, cosine, sine, starts, back):
    count, depth = x.shape
    width = weights.shape[2]
    return pl.pallas_call(
        functools.partial(attend_kernel, n),
        name="attention_forward",
        out_shape=(
            jax.ShapeDtypeStruct((count, depth), BF),
            jax.ShapeDtypeStruct((3, count, width), BF),
            jax.ShapeDtypeStruct((count, width), BF),
            jax.ShapeDtypeStruct((width // HEAD_DIM, count), F32),
            jax.ShapeDtypeStruct((count, LANES), F32),
            jax.ShapeDtypeStruct((n,) + back.shape, BF),
        ),
        in_specs=[ANY, WHOLE, ANY, WHOLE, WHOLE, WHOLE, ANY],
        out_specs=(ANY, ANY, ANY, WHOLE, WHOLE, ANY),
        scratch_shapes=gather_sems(n, CHUNKS)
        + [
            pltpu.SemaphoreType.DMA,
            pltpu.VMEM((count, depth), BF),
            pltpu.VMEM(weights.shape, BF),
            pltpu.VMEM((count, depth), BF),
            pltpu.VMEM((3, count, width), BF),
            pltpu.VMEM((count, width), BF),
            pltpu.SemaphoreType.DMA((5,)),
        ],
        compiler_params=params(2),
        cost_estimate=cost(65),
    )(x, gain, weights, cosine, sine, starts, back)


def branch_kernel(
    n, att_ref, w_hbm, x_hbm, gain_ref, h_ref, hidden_ref, held, total, send, recv, w_ref, x_ref, load_sem
):
    me = lax.axis_index("tensor")
    count, width = att_ref.shape
    rows_each = hidden_ref.shape[0]
    size = count // CHUNKS
    loads = (
        pltpu.make_async_copy(w_hbm, w_ref, load_sem.at[0]),
        pltpu.make_async_copy(x_hbm, x_ref, load_sem.at[1]),
    )
    for copy in loads:
        copy.start()
    chain_barrier(me, n)
    gather = Gather(
        me,
        n,
        lambda c: att_ref.at[pl.ds(c * size, size)],
        lambda shard, c: held.at[shard, pl.ds(c * size, size)],
        send,
        recv,
        CHUNKS,
    )
    gather.start()

    def add(source, shard, first, start, stop):
        weights = pl.ds(pl.multiple_of(shard * width, width), width)

        def tile(r, carry):
            rows = pl.ds(pl.multiple_of(r * TILE, TILE), TILE)
            term = nn(source[rows], w_ref[weights])
            total[rows] = term + (x_ref[rows].astype(F32) if first else total[rows])
            return carry

        lax.fori_loop(start // TILE, stop // TILE, tile, 0)

    def arrived(step, start, stop):
        for way in range(2):

            @pl.when(gather.holds(way, step))
            def _(way=way):
                shard = me - step if way == 0 else me + step
                add(held.at[shard], shard, False, start, stop)

    def norm(r, carry):
        rows = pl.ds(pl.multiple_of(r * LANES, LANES), LANES)
        hidden = total[rows]
        h_ref[rows] = (hidden * row_scale(hidden) * gain_ref[1:2]).astype(BF)
        return carry

    for copy in loads:
        copy.wait()
    add(att_ref, me, True, 0, count)
    for step in range(1, n - 1):
        gather.advance(step)
        arrived(step, 0, count)
    for c in range(CHUNKS):
        gather.advance(n - 1, c)
        arrived(n - 1, c * size, (c + 1) * size)
        lax.fori_loop(c * size // LANES, (c + 1) * size // LANES, norm, 0)
    hidden_ref[...] = total[pl.ds(pl.multiple_of(me * rows_each, rows_each), rows_each)]
    gather.finish()


def project_branch(n, att, weights, x, gain):
    count, width = att.shape
    depth = x.shape[1]
    return pl.pallas_call(
        functools.partial(branch_kernel, n),
        name="branch",
        out_shape=(
            jax.ShapeDtypeStruct((count, depth), BF),
            jax.ShapeDtypeStruct((count // n, depth), F32),
        ),
        in_specs=[WHOLE, ANY, ANY, WHOLE],
        out_specs=(WHOLE, WHOLE),
        scratch_shapes=[pltpu.VMEM((n, count, width), BF), pltpu.VMEM((count, depth), F32)]
        + gather_sems(n, CHUNKS)
        + [
            pltpu.VMEM((depth, depth), BF),
            pltpu.VMEM(x.shape, BF),
            pltpu.SemaphoreType.DMA((2,)),
        ],
        compiler_params=params(3),
        cost_estimate=cost(70),
    )(att, weights, x, gain)


def feed_kernel(
    n,
    h_hbm,
    back_hbm,
    w_hbm,
    inner_hbm,
    both_hbm,
    own_ref,
    part,
    inbox,
    send,
    recv,
    w,
    inner_ref,
    both,
    h_rows,
    back_rows,
    w_sem,
    row_sem,
    store_sem,
):
    me = lax.axis_index("tensor")
    rows_each, depth = own_ref.shape
    hidden = inner_ref.shape[1]
    tiles = hidden // TILE
    pair = 2 if tiles % 2 == 0 else 1

    def fetch(b):
        cols = pl.ds(pl.multiple_of(b * TILE, TILE), TILE)
        return pltpu.make_async_copy(w_hbm.at[:, :, cols], w.at[:, :, cols], w_sem.at[b])

    def fetch_rows(dest):
        rows = pl.ds(pl.multiple_of(dest * rows_each, rows_each), rows_each)
        return (
            pltpu.make_async_copy(h_hbm.at[rows], h_rows, row_sem.at[0]),
            pltpu.make_async_copy(back_hbm.at[rows], back_rows, row_sem.at[1]),
        )

    def stores(i, dest):
        rows = pl.ds(pl.multiple_of(dest * rows_each, rows_each), rows_each)
        return (
            pltpu.make_async_copy(inner_ref.at[rows], inner_hbm.at[rows], store_sem.at[i, 0]),
            pltpu.make_async_copy(both.at[:, rows], both_hbm.at[:, rows], store_sem.at[i, 1]),
        )

    for copy in fetch_rows(nth_dest(me, n, 0)):
        copy.start()
    for b in range(tiles):
        fetch(b).start()
    chain_barrier(me, n)
    scatter = Scatter(me, n, part, own_ref, inbox, send, recv, FINE)
    own_ref[...] = jnp.zeros_like(own_ref)
    step_cols = 512
    steps = tiles // pair
    per_block = steps + depth // step_cols
    last = n * per_block
    due = [last + 1] * scatter.events
    if n == 4 and per_block == 8:
        due = [11, 16, 17, 19, 24, 25, 26, 28, 31] + due[9:]

    def serve(tick):
        def count(now):
            return functools.reduce(jnp.add, [(now >= at).astype(jnp.int32) for at in due])

        scatter.relays(count(tick - 1), count(tick))

    for i in range(n):
        dest = nth_dest(me, n, i)
        rows = pl.ds(pl.multiple_of(dest * rows_each, rows_each), rows_each)
        for copy in fetch_rows(dest):
            copy.wait()

        def forward(b, carry, i=i, rows=rows):
            if i == 0:
                for half in range(pair):
                    fetch(pair * b + half).wait()
            for half in range(pair):
                cols = pl.ds(pl.multiple_of((pair * b + half) * TILE, TILE), TILE)
                gate = nn(h_rows[...], w[0, :, cols])
                up = nn(h_rows[...], w[1, :, cols])
                d_inner = nn(back_rows[...], w[2, :, cols])
                sigmoid = jax.nn.sigmoid(gate)
                silu = gate * sigmoid
                inner_ref[rows, cols] = (silu * up).astype(BF)
                both[0, rows, cols] = (d_inner * up * sigmoid * (1.0 + gate * (1.0 - sigmoid))).astype(BF)
                both[1, rows, cols] = (d_inner * silu).astype(BF)
            if i > 0:
                serve(i * per_block + 1 + b)
            return carry

        lax.fori_loop(0, steps, forward, 0)
        if i < n - 1:
            for copy in fetch_rows(nth_dest(me, n, i + 1)):
                copy.start()
        for copy in stores(i, dest):
            copy.start()

        def backward(c, carry, i=i, rows=rows, dest=dest):
            cols = pl.ds(pl.multiple_of(c * step_cols, step_cols), step_cols)
            value = nt(both[0, rows], w[0, cols]) + nt(both[1, rows], w[1, cols])
            if i < n - 1:
                part[dest, :, cols] = value.astype(BF)
            else:
                own_ref[:, cols] = own_ref[:, cols] + value
            if i > 0:
                serve(i * per_block + steps + 1 + c)
            return carry

        lax.fori_loop(0, depth // step_cols, backward, 0)
        if i < n - 1:
            scatter.offer(dest)

    late = [at for at in range(scatter.events) if due[at] > last]
    scatter.relays(late[0], scatter.events)
    for i in range(n):
        for copy in stores(i, nth_dest(me, n, i)):
            copy.wait()
    scatter.finish()


def feed(n, h, back, weights):
    count, depth = h.shape
    hidden = weights.shape[2]
    rows = count // n
    return pl.pallas_call(
        functools.partial(feed_kernel, n),
        name="feed_forward",
        out_shape=(
            jax.ShapeDtypeStruct((count, hidden), BF),
            jax.ShapeDtypeStruct((2, count, hidden), BF),
            jax.ShapeDtypeStruct((rows, depth), F32),
        ),
        in_specs=[ANY] * 3,
        out_specs=(ANY, ANY, WHOLE),
        scratch_shapes=scatter_scratch(n, rows, depth, FINE)
        + [
            pltpu.VMEM((3, depth, hidden), BF),
            pltpu.VMEM((count, hidden), BF),
            pltpu.VMEM((2, count, hidden), BF),
            pltpu.VMEM((rows, depth), BF),
            pltpu.VMEM((rows, depth), BF),
            pltpu.SemaphoreType.DMA((hidden // TILE,)),
            pltpu.SemaphoreType.DMA((2,)),
            pltpu.SemaphoreType.DMA((n, 2)),
        ],
        compiler_params=params(4),
        cost_estimate=cost(95),
    )(h, back, weights)


def branch_back_kernel(
    n,
    m,
    d_two_ref,
    hidden_ref,
    cot_ref,
    gain_ref,
    w_hbm,
    h_hbm,
    both_hbm,
    back_hbm,
    inner_hbm,
    feed_hbm,
    d_hidden_ref,
    d_att_ref,
    gain_part_ref,
    all_hbm,
    grad_hbm,
    down_ref,
    first_ref,
    held,
    w_ref,
    send,
    recv,
    w_sem,
    out_sem,
    both,
    inner,
    h_cols,
    back_cols,
    slot,
    both_sem,
    col_sem,
    slot_sem,
    down,
    part,
    inbox,
    s_send,
    s_recv,
    *chip_scratch,
):
    me = lax.axis_index("tensor")
    line = lax.axis_index("dp")
    down_sum = ChipScatter(line, m, False, *chip_scratch)
    rows_each, depth = hidden_ref.shape
    width = d_att_ref.shape[1]
    size = rows_each // CHUNKS
    fetch = pltpu.make_async_copy(
        w_hbm.at[pl.ds(pl.multiple_of(me * width, width), width)], w_ref, w_sem
    )
    fetch.start()
    loads = (
        pltpu.make_async_copy(inner_hbm, inner, both_sem.at[0]),
        pltpu.make_async_copy(feed_hbm.at[2, pl.ds(0, down.shape[0])], down, both_sem.at[1]),
        pltpu.make_async_copy(both_hbm, both, both_sem.at[2]),
    )
    for copy in loads:
        copy.start()
    each = depth // m

    def fetch_cols(at):
        cols = pl.ds(pl.multiple_of(at * each, each), each)
        to = lax.rem(at, 2)
        return pltpu.make_async_copy(h_hbm.at[:, cols], h_cols.at[to], col_sem.at[0, to])

    def fetch_back(at):
        cols = pl.ds(pl.multiple_of(down_sum.target(at) * each, each), each)
        return pltpu.make_async_copy(back_hbm.at[:, cols], back_cols.at[at % 2], col_sem.at[1, at % 2])

    fetch_cols(0).start()
    fetch_back(0).start()
    chips_barrier(me, n, line, m)
    step_rows = min(LANES, rows_each)
    gain_part_ref[...] = jnp.zeros_like(gain_part_ref)

    def norm(r, carry):
        rows = pl.ds(pl.multiple_of(r * step_rows, step_rows), step_rows)
        hidden = hidden_ref[rows]
        scale = row_scale(hidden)
        normed = hidden * scale
        d_two = d_two_ref[rows]
        scaled = d_two * gain_ref[1:2]
        back = scale * (scaled - normed * jnp.mean(scaled * normed, axis=-1, keepdims=True))
        d_hidden = cot_ref[rows].astype(F32) + back
        d_hidden_ref[rows] = d_hidden
        held[me, rows] = d_hidden.astype(BF)
        gain_part_ref[1:2] = gain_part_ref[1:2] + jnp.sum(d_two * normed, axis=0, keepdims=True)
        return carry

    lax.fori_loop(0, rows_each // step_rows, norm, 0)

    gather = Gather(
        me,
        n,
        lambda c: held.at[me, pl.ds(c * size, size)],
        lambda shard, c: held.at[shard, pl.ds(c * size, size)],
        send,
        recv,
        CHUNKS,
    )
    gather.start()

    def use(shard):
        rows = pl.ds(pl.multiple_of(shard * rows_each, rows_each), rows_each)
        pltpu.make_async_copy(held.at[shard], all_hbm.at[shard], out_sem.at[shard]).start()
        d_att_ref[rows] = nt(held[shard], w_ref[...]).astype(BF)

    def out_copy(at, kind):
        return pltpu.make_async_copy(slot.at[kind], grad_hbm.at[2 * at + kind], slot_sem.at[kind])

    step_cols = 512
    tiles = inner.shape[1] // step_cols

    def up_piece(at, carry):
        @pl.when(at + 1 < m)
        def _():
            fetch_cols(at + 1).start()

        fetch_cols(at).wait()
        turned = jnp.transpose(h_cols[lax.rem(at, 2)])
        for kind in range(2):

            @pl.when(at > 0)
            def _(kind=kind):
                out_copy(at - 1, kind).wait()

            def tile(c, inner_carry, kind=kind):
                cols = pl.ds(pl.multiple_of(c * step_cols, step_cols), step_cols)
                slot[kind, :, cols] = nn(turned, both[kind, :, cols]).astype(BF)
                return inner_carry

            lax.fori_loop(0, tiles, tile, 0)
            out_copy(at, kind).start()
        return carry

    def down_piece(at):
        if at + 1 < m:
            fetch_back(at + 1).start()
        fetch_back(at).wait()
        turned = jnp.transpose(back_cols[at % 2])
        to = down_sum.slot(at)

        def tile(c, carry):
            cols = pl.ds(pl.multiple_of(c * step_cols, step_cols), step_cols)
            to[0, :, cols] = nn(turned, inner[:, cols]).astype(BF)
            return carry

        lax.fori_loop(0, tiles, tile, 0)
        down_sum.filled(at)

    scatter = Scatter(me, n, part, first_ref, inbox, s_send, s_recv, CHUNKS)
    first_ref[...] = hidden_ref[:, 0 : first_ref.shape[1]]
    loads[0].wait()
    loads[1].wait()
    for i in range(n):
        dest = nth_dest(me, n, i)
        rows = pl.ds(pl.multiple_of(dest * rows_each, rows_each), rows_each)
        value = nt(inner[rows], down[...])
        if i < n - 1:
            part[dest] = value.astype(BF)
            scatter.offer(dest)
        else:
            first_ref[...] = first_ref[...] + value
    for at in range(m):
        down_piece(at)
    fetch.wait()
    use(me)
    down_sum.combine(0)
    down_sum.forward()
    loads[2].wait()

    def arrived(step):
        for way in range(2):

            @pl.when(gather.holds(way, step))
            def _(way=way):
                use(me - step if way == 0 else me + step)

    gather.advance(1)
    arrived(1)
    lax.fori_loop(0, m // 2, up_piece, 0)
    gather.advance(2)
    arrived(2)
    lax.fori_loop(m // 2, m, up_piece, 0)
    scatter.relays(0, scatter.events)
    for step in range(3, n):
        gather.advance(step)
        arrived(step)
    down_sum.arrive()
    down_ref[...] = jnp.transpose(down_sum.result(0))
    for kind in range(2):
        out_copy(m - 1, kind).wait()
    for shard in range(n):
        pltpu.make_async_copy(held.at[shard], all_hbm.at[shard], out_sem.at[shard]).wait()
    gather.finish()
    scatter.finish()
    down_sum.finish()


def branch_back(n, m, d_two, hidden, cotangent, gain, out_weights, h, both, back, inner, feed_weights, width):
    rows, depth = hidden.shape
    _, count, inner_width = both.shape
    each = depth // m
    first = depth // FIRST
    return pl.pallas_call(
        functools.partial(branch_back_kernel, n, m),
        name="branch_backward",
        out_shape=(
            jax.ShapeDtypeStruct((rows, depth), F32),
            jax.ShapeDtypeStruct((n * rows, width), BF),
            jax.ShapeDtypeStruct((8, depth), F32),
            jax.ShapeDtypeStruct((n, rows, depth), BF),
            jax.ShapeDtypeStruct((2 * m, each, inner_width), BF),
            jax.ShapeDtypeStruct((inner_width, each), F32),
            jax.ShapeDtypeStruct((rows, first), F32),
        ),
        in_specs=[WHOLE] * 4 + [ANY] * 6,
        out_specs=(WHOLE, WHOLE, WHOLE, ANY, ANY, WHOLE, WHOLE),
        scratch_shapes=[pltpu.VMEM((n, rows, depth), BF), pltpu.VMEM((width, depth), BF)]
        + gather_sems(n, CHUNKS)
        + [
            pltpu.SemaphoreType.DMA,
            pltpu.SemaphoreType.DMA((n,)),
            pltpu.VMEM(both.shape, BF),
            pltpu.VMEM(inner.shape, BF),
            pltpu.VMEM((2, count, each), BF),
            pltpu.VMEM((2, count, each), BF),
            pltpu.VMEM((2, each, inner_width), BF),
            pltpu.SemaphoreType.DMA((3,)),
            pltpu.SemaphoreType.DMA((2, 2)),
            pltpu.SemaphoreType.DMA((2,)),
            pltpu.VMEM((first, inner_width), BF),
        ]
        + scatter_scratch(n, rows, first, CHUNKS)
        + chip_scatter_scratch(m, (1, each, inner_width)),
        compiler_params=params(5),
        cost_estimate=cost(75),
    )(d_two, hidden, cotangent, gain, out_weights, h, both, back, inner, feed_weights)


def attend_back_kernel(
    n,
    lse_ref,
    start_ref,
    qkv_hbm,
    d_att_hbm,
    cos_hbm,
    sin_hbm,
    hidden_hbm,
    inner_hbm,
    w_hbm,
    first_ref,
    d_hbm,
    out_ref,
    part,
    inbox,
    send,
    recv,
    own,
    inner,
    down,
    key_sum,
    value_sum,
    load_sem,
    qkv_ref,
    d_att_ref,
    cos_ref,
    sin_ref,
    d_ref,
    store_sem,
):
    me = lax.axis_index("tensor")
    count, width = d_att_ref.shape
    rows_each, depth = out_ref.shape
    first = first_ref.shape[1]
    blocks = count // TILE
    loads = [
        pltpu.make_async_copy(src, dst, load_sem.at[at])
        for at, (src, dst) in enumerate(
            (
                (hidden_hbm.at[:, pl.ds(first, depth - first)], own),
                (inner_hbm, inner),
                (w_hbm.at[2, pl.ds(first, depth - first)], down),
                (qkv_hbm, qkv_ref),
                (d_att_hbm, d_att_ref),
                (cos_hbm, cos_ref),
                (sin_hbm, sin_ref),
            )
        )
    ]
    for copy in loads:
        copy.start()

    chain_barrier(me, n)
    scatter = Scatter(me, n, part, own, inbox, send, recv, FINE)
    for copy in loads[:3]:
        copy.wait()
    step_cols = 512
    for i in range(n):
        dest = nth_dest(me, n, i)

        def tile(c, carry, i=i, dest=dest):
            rows = pl.ds(pl.multiple_of(dest * rows_each, rows_each), rows_each)
            cols = pl.ds(pl.multiple_of(c * step_cols, step_cols), step_cols)
            value = nt(inner[rows], down[cols])
            if i < n - 1:
                part[dest, :, cols] = value.astype(BF)
            else:
                own[:, cols] = own[:, cols] + value
            return carry

        lax.fori_loop(0, (depth - first) // step_cols, tile, 0)
        if i < n - 1:
            scatter.offer(dest)
    for copy in loads[3:]:
        copy.wait()

    lane = lax.broadcasted_iota(jnp.int32, (TILE, LANES), 1)
    key_row = lax.broadcasted_iota(jnp.int32, (TILE, TILE), 0)
    query_lane = lax.broadcasted_iota(jnp.int32, (TILE, TILE), 1)
    diagonal = key_row <= query_lane
    scale = HEAD_DIM ** (-0.5)

    def unrotate(value, rows):
        return value * cos_ref[rows] - half_swap(value) * sin_ref[rows]

    def pair(p, carry):
        cols = pl.ds(pl.multiple_of(p * LANES, LANES), LANES)
        key_sum[...] = jnp.zeros_like(key_sum)
        value_sum[...] = jnp.zeros_like(value_sum)
        for i in range(blocks):
            rows = pl.ds(i * TILE, TILE)
            query = qkv_ref[0, rows, cols] * jnp.asarray(scale, BF)
            back = d_att_ref[rows, cols]
            begin = start_ref[0:1, rows]
            query_grad = jnp.zeros((TILE, LANES), F32)
            for e in range(2):
                ours = lane < HEAD_DIM if e == 0 else lane >= HEAD_DIM
                q = jnp.where(ours, query, jnp.zeros_like(query))
                d = jnp.where(ours, back, jnp.zeros_like(back))
                lse = lse_ref[pl.ds(2 * p + e, 1), rows]
                probs, d_probs = [], []
                centre = jnp.zeros((1, TILE), F32)
                for j in range(i + 1):
                    keys = pl.ds(j * TILE, TILE)
                    s = nt(qkv_ref[1, keys, cols], q)
                    allowed = key_row >= begin - j * TILE
                    if j == i:
                        allowed = allowed & diagonal
                    prob = jnp.where(allowed, jnp.exp(s - lse), 0.0)
                    d_prob = nt(qkv_ref[2, keys, cols], d)
                    centre = centre + jnp.sum(prob * d_prob, axis=0, keepdims=True)
                    value_sum[keys] = value_sum[keys] + nn(prob.astype(BF), d)
                    probs.append(prob)
                    d_probs.append(d_prob)
                for j in range(i + 1):
                    keys = pl.ds(j * TILE, TILE)
                    d_score = (probs[j] * (d_probs[j] - centre)).astype(BF)
                    key_sum[keys] = key_sum[keys] + nn(d_score, q)
                    k = qkv_ref[1, keys, cols]
                    query_grad = query_grad + tn(d_score, jnp.where(ours, k, jnp.zeros_like(k)))
            d_ref[0, rows, cols] = unrotate(query_grad * scale, rows).astype(BF)
            if i == blocks // 2 - 1:
                scatter.relays(5 * p // 2, 5 * p // 2 + 1)
            if i == blocks // 2:
                scatter.relays(5 * p // 2 + 1, 5 * (p + 1) // 2 - 1)
        for i in range(blocks):
            rows = pl.ds(i * TILE, TILE)
            d_ref[1, rows, cols] = unrotate(key_sum[rows], rows).astype(BF)
            d_ref[2, rows, cols] = value_sum[rows].astype(BF)
        scatter.relays(5 * (p + 1) // 2 - 1, 5 * (p + 1) // 2)
        return carry

    pairs = width // LANES
    lax.fori_loop(0, pairs, pair, 0)
    done = 5 * pairs // 2

    store = pltpu.make_async_copy(d_ref, d_hbm, store_sem)
    store.start()
    scatter.relays(done, scatter.events)
    out_ref[:, 0:first] = first_ref[...].astype(BF)
    out_ref[:, first:depth] = own[...].astype(BF)
    scatter.finish()
    store.wait()


def attend_back(n, qkv, d_att, lse, starts, cosine, sine, hidden, inner, weights, feed_first):
    _, count, width = qkv.shape
    rows, depth = hidden.shape
    inner_width = inner.shape[1]
    rest = depth - feed_first.shape[1]
    return pl.pallas_call(
        functools.partial(attend_back_kernel, n),
        name="attention_backward",
        out_shape=(
            jax.ShapeDtypeStruct((3, count, width), BF),
            jax.ShapeDtypeStruct((rows, depth), BF),
        ),
        in_specs=[WHOLE] * 2 + [ANY] * 7 + [WHOLE],
        out_specs=(ANY, WHOLE),
        scratch_shapes=scatter_scratch(n, rows, rest, FINE)
        + [
            pltpu.VMEM((rows, rest), F32),
            pltpu.VMEM((count, inner_width), BF),
            pltpu.VMEM((rest, inner_width), BF),
            pltpu.VMEM((count, LANES), F32),
            pltpu.VMEM((count, LANES), F32),
            pltpu.SemaphoreType.DMA((7,)),
            pltpu.VMEM(qkv.shape, BF),
            pltpu.VMEM(d_att.shape, BF),
            pltpu.VMEM(cosine.shape, F32),
            pltpu.VMEM(sine.shape, F32),
            pltpu.VMEM(qkv.shape, BF),
            pltpu.SemaphoreType.DMA,
        ],
        compiler_params=params(6),
        cost_estimate=cost(80),
    )(
        lse,
        starts,
        qkv,
        d_att,
        cosine,
        sine,
        hidden,
        inner,
        weights,
        feed_first,
    )


def input_back_kernel(
    n,
    m,
    d_ref,
    w_ref,
    x_ref,
    gain_ref,
    d_hidden_ref,
    gain_two_ref,
    scale_ref,
    all_x_hbm,
    h_hbm,
    branch_hbm,
    att_hbm,
    grad_ref,
    in_ref,
    out_ref,
    gain_ref_out,
    part,
    inbox,
    send,
    recv,
    own,
    gain_part,
    t_box,
    line_sum,
    d_box,
    t_send,
    t_recv,
    d_send,
    d_recv,
    att,
    h_cols,
    branch_cols,
    all_x,
    att_sem,
    x_sem,
    col_sem,
    *chip_scratch,
):
    me = lax.axis_index("tensor")
    line = lax.axis_index("dp")
    rows_each, depth = x_ref.shape
    kinds = in_ref.shape[0] + 1
    mixed_sum = ChipScatter(line, m, True, *chip_scratch)
    each = in_ref.shape[1]
    fetch_att = pltpu.make_async_copy(att_hbm, att, att_sem)
    fetch_x = pltpu.make_async_copy(all_x_hbm, all_x, x_sem)
    fetch_x.start()
    fetch_att.start()

    def fetch_cols(at):
        cols = pl.ds(pl.multiple_of(mixed_sum.target(at) * each, each), each)
        return (
            pltpu.make_async_copy(h_hbm.at[:, cols], h_cols.at[at % 2], col_sem.at[0, at % 2]),
            pltpu.make_async_copy(branch_hbm.at[:, cols], branch_cols.at[at % 2], col_sem.at[1, at % 2]),
        )

    for copy in fetch_cols(0):
        copy.start()
    everyone_barrier(me, n, line, m)
    scatter = Scatter(me, n, part, own, inbox, send, recv, FINE)
    own[...] = jnp.zeros_like(own)
    gain_part[...] = gain_two_ref[...]
    fetch_x.wait()
    step_cols = 512

    def term(i):
        dest = nth_dest(me, n, i)

        def tile(c, carry):
            rows = pl.ds(pl.multiple_of(dest * rows_each, rows_each), rows_each)
            cols = pl.ds(pl.multiple_of(c * step_cols, step_cols), step_cols)
            value = nt(d_ref[0, rows], w_ref[0, cols])
            for kind in range(1, 3):
                value = value + nt(d_ref[kind, rows], w_ref[kind, cols])
            if i < n - 1:
                part[dest, :, cols] = value.astype(BF)
            else:
                own[:, cols] = own[:, cols] + value
            normed = all_x[rows, cols].astype(F32) * scale_ref[rows, 0:1]
            gain_part[0:1, cols] = gain_part[0:1, cols] + jnp.sum(value * normed, axis=0, keepdims=True)
            return carry

        lax.fori_loop(0, depth // step_cols, tile, 0)
        if i < n - 1:
            scatter.offer(dest)

    term(0)
    term(1)
    def across(hop):
        return pltpu.make_async_remote_copy(
            src_ref=gain_part,
            dst_ref=t_box.at[hop],
            send_sem=t_send.at[hop],
            recv_sem=t_recv.at[hop],
            device_id={"tensor": lax.rem(me + hop, n)},
            device_id_type=MESH,
        )

    def along(hop):
        to = lax.rem(line + hop, m)
        return pltpu.make_async_remote_copy(
            src_ref=line_sum.at[to],
            dst_ref=d_box.at[hop],
            send_sem=d_send.at[hop],
            recv_sem=d_recv.at[hop],
            device_id={"dp": to},
            device_id_type=MESH,
        )

    fetch_att.wait()
    served = 0
    for at in range(m):
        if at + 1 < m:
            for copy in fetch_cols(at + 1):
                copy.start()
        for copy in fetch_cols(at):
            copy.wait()
        h_turned = jnp.transpose(h_cols[at % 2])
        branch_turned = jnp.transpose(branch_cols[at % 2])
        to = mixed_sum.slot(at)
        for kind in range(kinds):
            value = nn(h_turned, d_ref[kind]) if kind < kinds - 1 else nn(branch_turned, att[...])
            to[kind] = value.astype(BF)
        mixed_sum.filled(at)
        if 4 * (at + 1) // m - 1 > served:
            scatter.relay(served)
            served += 1
        if at == m // 2 - 1:
            for i in range(2, n - 1):
                term(i)
    mixed_sum.forward()
    mixed_sum.combine(0)
    term(n - 1)
    for hop in range(1, n):
        across(hop).start()
    scatter.relays(served, served + 3)
    for hop in range(1, n):
        across(hop).wait_recv()
    gain_total = gain_part[...]
    for hop in range(1, n):
        gain_total = gain_total + t_box[hop]
    gain_width = gain_ref_out.shape[1]
    for at in range(m):
        line_sum[at] = gain_total[:, at * gain_width : (at + 1) * gain_width]
    for hop in range(1, m):
        along(hop).start()
    scatter.relays(served + 3, scatter.events)
    step_rows = min(LANES, rows_each)

    def norm(r, carry):
        rows = pl.ds(pl.multiple_of(r * step_rows, step_rows), step_rows)
        x = x_ref[rows].astype(F32)
        scale = row_scale(x)
        normed = x * scale
        d_one = own[rows]
        scaled = d_one * gain_ref[0:1]
        back = scale * (scaled - normed * jnp.mean(scaled * normed, axis=-1, keepdims=True))
        grad_ref[rows] = d_hidden_ref[rows] + back
        return carry

    lax.fori_loop(0, rows_each // step_rows, norm, 0)
    for hop in range(1, m):
        along(hop).wait_recv()
    result = line_sum[line]
    for hop in range(1, m):
        result = result + d_box[hop]
    gain_ref_out[...] = result
    mixed_sum.arrive()
    for kind in range(kinds):
        total = mixed_sum.result(kind)
        if kind < kinds - 1:
            in_ref[kind] = total
        else:
            out_ref[...] = jnp.transpose(total)

    scatter.finish()
    for hop in range(1, n):
        across(hop).wait_send()
    for hop in range(1, m):
        along(hop).wait_send()
    mixed_sum.finish()


def input_back(
    n, m, d_projected, weights, x, gain, d_hidden, gain_two, scale, all_x, h, d_branch, attended
):
    rows, depth = x.shape
    kinds = d_projected.shape[0] + 1
    each = depth // m
    count, width = attended.shape
    shard = (kinds, each, width)
    return pl.pallas_call(
        functools.partial(input_back_kernel, n, m),
        name="input_backward",
        out_shape=(
            jax.ShapeDtypeStruct((rows, depth), F32),
            jax.ShapeDtypeStruct((kinds - 1, each, width), F32),
            jax.ShapeDtypeStruct((width, each), F32),
            jax.ShapeDtypeStruct((8, each), F32),
        ),
        in_specs=[WHOLE] * 7 + [ANY] * 4,
        out_specs=(WHOLE,) * 4,
        scratch_shapes=scatter_scratch(n, rows, depth, FINE)
        + [pltpu.VMEM((rows, depth), F32)]
        + [
            pltpu.VMEM((8, depth), F32),
            pltpu.VMEM((n, 8, depth), F32),
            pltpu.VMEM((m, 8, each), F32),
            pltpu.VMEM((m, 8, each), F32),
            pltpu.SemaphoreType.DMA((n,)),
            pltpu.SemaphoreType.DMA((n,)),
            pltpu.SemaphoreType.DMA((m,)),
            pltpu.SemaphoreType.DMA((m,)),
            pltpu.VMEM((count, width), BF),
            pltpu.VMEM((2, count, each), BF),
            pltpu.VMEM((2, count, each), BF),
            pltpu.VMEM((count, depth), BF),
            pltpu.SemaphoreType.DMA,
            pltpu.SemaphoreType.DMA,
            pltpu.SemaphoreType.DMA((2, 2)),
        ]
        + chip_scatter_scratch(m, shard),
        compiler_params=params(7),
        cost_estimate=cost(75),
    )(
        d_projected,
        weights,
        x,
        gain,
        d_hidden,
        gain_two,
        scale,
        all_x,
        h,
        d_branch,
        attended,
    )


def adam_kernel(rate, decay, w_ref, first_ref, second_ref, grad_ref, first_out, second_out, w_out):
    for kind in range(2):
        new = adam_step(
            w_ref[:, kind, :],
            first_ref[:, kind, :],
            second_ref[:, kind, :],
            grad_ref[kind].astype(F32),
            rate,
            decay,
        )
        first_out[:, kind, :] = new[0]
        second_out[:, kind, :] = new[1]
        w_out[:, kind, :] = new[2]


def adam_pair(weight, first, second, grad, rate, decay):
    rows, kinds, width = weight.shape
    step = 64
    spec = pl.BlockSpec((step, kinds, width), lambda i: (i, 0, 0))
    shape = jax.ShapeDtypeStruct(weight.shape, F32)
    return pl.pallas_call(
        functools.partial(adam_kernel, rate, decay),
        name="adam_gate_up",
        grid=(rows // step,),
        out_shape=(shape,) * 3,
        in_specs=[spec] * 3 + [pl.BlockSpec((kinds, step, width), lambda i: (0, i, 0))],
        out_specs=(spec,) * 3,
        compiler_params=params(),
        cost_estimate=cost(10),
    )(weight, first, second, grad)


def rows_first(array):
    return with_layout_constraint(array, Layout(major_to_minor=tuple(range(array.ndim))))


def adam_step(weight, first_moment, second_moment, grad, rate, decay):
    new_first = BETA_ONE * first_moment + (1.0 - BETA_ONE) * grad
    new_second = BETA_TWO * second_moment + (1.0 - BETA_TWO) * grad * grad
    mean_part = new_first / (1.0 - BETA_ONE**STEP)
    size_part = jnp.sqrt(new_second / (1.0 - BETA_TWO**STEP)) + ADAM_EPSILON
    new_weight = weight - rate * (mean_part / size_part + decay * weight)
    return (new_first, new_second, new_weight)


def local(
    n,
    m,
    tokens,
    cotangent,
    doc_start,
    in_weight,
    in_first,
    in_second,
    out_weight,
    out_first,
    out_second,
    gate_up,
    gate_up_first,
    gate_up_second,
    down_weight,
    down_first,
    down_second,
    norm_gains,
    gains_first,
    gains_second,
):
    count = doc_start.shape[0]
    depth = tokens.shape[1]

    in_low = jnp.transpose(in_weight, (1, 0, 2)).astype(BF)
    gain_low = jnp.pad(lax.reduce_precision(norm_gains, 8, 7), ((0, 6), (0, 0)))
    powers = jnp.arange(HEAD_DIM // 2, dtype=F32) * (2.0 / HEAD_DIM)
    freqs = jnp.broadcast_to(jnp.tile(ROPE_BASE ** (-powers), 4)[None, :], (8, LANES))
    start_rows = jnp.broadcast_to(doc_start[:, None], (count, LANES))
    start_lanes = jnp.broadcast_to(doc_start[None, :], (8, count))

    in_w = lax.all_gather(in_low, "dp", axis=1, tiled=True)
    out_line, gain_line = gather_first(n, m, out_weight.astype(BF), gain_low)
    gains = jnp.transpose(gain_line, (1, 0, 2)).reshape(8, depth)
    out_line = out_line.reshape(depth, out_line.shape[2])
    out_w = lax.all_gather(out_line, "dp", axis=1, tiled=True)

    own_tokens, _ = lax.optimization_barrier((tokens, gains))
    x, feed_low, cosine, sine = gather_rows(n, own_tokens, gate_up, down_weight, start_rows, freqs)
    x = x.reshape(count, depth)
    feed_w = lax.all_gather(feed_low, "dp", axis=1, tiled=True)

    h_one, qkv, attended, lse, scale_one, back = attend(
        n, x, gains, in_w, cosine, sine, start_rows, cotangent
    )
    back = back.reshape(count, depth)
    h_two, hidden = project_branch(n, attended, out_w, x, gains)
    inner, d_both, d_two = feed(n, h_two, back, feed_w)
    d_hidden, d_att, gain_two, d_branch, up_grad, down_summed, feed_first = branch_back(
        n,
        m,
        d_two,
        hidden,
        cotangent,
        gains,
        out_w,
        h_two,
        d_both,
        back,
        inner,
        feed_w,
        attended.shape[1],
    )
    up_summed = rows_first(lax.psum_scatter(up_grad, "dp", scatter_dimension=0, tiled=True))
    d_projected, output = attend_back(
        n, qkv, d_att, lse, start_lanes, cosine, sine, hidden, inner, feed_w, feed_first
    )
    input_grad, in_summed, out_summed, gain_summed = input_back(
        n,
        m,
        d_projected,
        in_w,
        tokens,
        gains,
        d_hidden,
        gain_two,
        scale_one,
        x,
        h_one,
        d_branch.reshape(count, depth),
        attended,
    )
    up_new = tuple(
        adam_pair(
            gate_up, gate_up_first, gate_up_second, up_summed, 2.0 * D ** (-0.5), WEIGHT_DECAY
        )
    )
    down_new = adam_step(
        down_weight, down_first, down_second, down_summed, 2.0 * FF ** (-0.5), WEIGHT_DECAY
    )
    in_new = adam_step(
        in_weight, in_first, in_second, jnp.transpose(in_summed, (1, 0, 2)), 2.0 * D ** (-0.5), WEIGHT_DECAY
    )
    out_new = adam_step(
        out_weight, out_first, out_second, out_summed, 2.0 * (D // 8) ** (-0.5), WEIGHT_DECAY
    )
    gain_new = adam_step(norm_gains, gains_first, gains_second, gain_summed[0:2], GAIN_RATE, 0.0)
    return (output, input_grad) + in_new + out_new + up_new + down_new + gain_new


def solution(mesh):
    rows = P(("dp", "tensor"), None)
    wide = P("dp", None, "tensor")
    tall = P("tensor", "dp")
    gains = P(None, "dp")
    in_specs = (rows, rows, P("dp")) + (wide,) * 3 + (tall,) * 3 + (wide,) * 3 + (tall,) * 3 + (gains,) * 3
    out_specs = (rows, rows) + (wide,) * 3 + (tall,) * 3 + (wide,) * 3 + (tall,) * 3 + (gains,) * 3
    return jax.shard_map(
        functools.partial(local, mesh.shape["tensor"], mesh.shape["dp"]),
        mesh=mesh,
        in_specs=in_specs,
        out_specs=out_specs,
        check_vma=False,
    )
```
